256 devices in a mesh: rows: 8 (over y, core), cols: 32 (over z, x).
Axes of the slice: x: 4, y: 4, z: 8, core: 2. Of those that a mesh axis runs over, the one named last changes fastest.
Arguments:
- noise: bfloat16 [32768, 256], P(('rows', 'cols')), may hold values from -24 to 24
- data: bfloat16 [32768, 256], P(('cols', 'rows')), may hold values from -6 to 6
Outputs:
- targets: float32 [32768, 256], P(('rows', 'cols'))
The draws below stay inside these ranges and needn't reach their ends.
All inputs are finite; a program needn't handle non-finite values.
Results may differ from the reference program's by a relative error of at most 0.00055.
Values may be sent and summed in bfloat16 or wider, within the bound.
A program may use at most 128 MiB of HBM per device.

```python
import math
import jax
import jax.numpy as jnp
from jax import lax

D = 256
NR_DEV = 4096
ITERS = 4
N = 32768
M = 32768


def shared_signs(key):
    return jax.random.rademacher(jax.random.fold_in(key, 99), (7, D), dtype=jnp.float32)


def draw_noise(key, part):
    signs = shared_signs(key)
    key = jax.random.fold_in(key, 1)
    common = 2.5 * signs[0][None, :]
    values = common + jnp.clip(jax.random.normal(key, (N, D), jnp.float32), -6.0, 6.0)
    return values.astype(jnp.bfloat16)


def draw_data(key, part):
    signs = shared_signs(key)
    key = jax.random.fold_in(key, 2)
    first = jax.random.fold_in(key, 0)
    third = jax.random.fold_in(key, 2)
    amount = jax.random.uniform(third, (M, 1), jnp.float32, 0.0, 3.0)
    common = amount * signs[0][None, :]
    values = common + jnp.clip(jax.random.normal(first, (M, D), jnp.float32), -3.0, 3.0)
    return jnp.clip(values, -6.0, 6.0).astype(jnp.bfloat16)


def setup_inputs(seed: int = 0) -> dict:
    splits = jax.random.split(jax.random.key(seed), 3)
    return {
        "noise": draw_noise(jax.random.fold_in(splits[2], 71), 0),
        "data": draw_data(jax.random.fold_in(splits[2], 71), 0),
    }


EPS = 0.5
INV_EPS = 2.0


def reference(noise, data):
    block = NR_DEV
    count = noise.shape[0] // block
    blocks = noise.reshape(count, block, D)
    log_a = -math.log(noise.shape[0])
    log_b = -math.log(data.shape[0])
    scale = D ** -0.5

    def scores(rows_block):
        return jnp.dot(rows_block, data.T, preferred_element_type=jnp.float32) * scale

    def row_update(g_vec):
        def one(rows_block):
            z_part = (g_vec[None, :] + scores(rows_block)) * INV_EPS
            top = jnp.max(z_part, 1)
            total = jnp.sum(jnp.exp(z_part - top[:, None]), 1)
            return EPS * (log_a - top - jnp.log(total))
        return lax.map(one, blocks).reshape(-1)

    def col_update(f_vec):
        f_blocks = f_vec.reshape(count, block)

        def step(carry, item):
            top, total = carry
            rows_block, f_part = item
            z_part = (f_part[:, None] + scores(rows_block)) * INV_EPS
            new_top = jnp.maximum(top, jnp.max(z_part, 0))
            total = total * jnp.exp(top - new_top) + jnp.sum(jnp.exp(z_part - new_top[None, :]), 0)
            return (new_top, total), None

        start = (jnp.full((data.shape[0],), -jnp.inf, jnp.float32), jnp.zeros((data.shape[0],), jnp.float32))
        (top, total), unused = lax.scan(step, start, (blocks, f_blocks))
        return EPS * (log_b - top - jnp.log(total))

    g_vec = jnp.zeros((data.shape[0],), jnp.float32)
    for step_index in range(ITERS):
        f_vec = row_update(g_vec)
        g_vec = col_update(f_vec)

    def final(rows_block):
        z_part = (g_vec[None, :] + scores(rows_block)) * INV_EPS
        top = jnp.max(z_part, 1)
        weights = jnp.exp(z_part - top[:, None]).astype(jnp.bfloat16)
        numerator = jnp.dot(weights, data, preferred_element_type=jnp.float32)
        denominator = jnp.sum(weights.astype(jnp.float32), 1)
        return numerator / denominator[:, None]

    return lax.map(final, blocks).reshape(noise.shape[0], D)
```

```python
import functools
import math

import jax
import jax.numpy as jnp
from jax import lax
from jax.experimental import pallas as pl
from jax.experimental.pallas import tpu as pltpu
from jax.sharding import PartitionSpec as P

MESH = pl.DeviceIdType.MESH
F32 = jnp.float32
BF16 = jnp.bfloat16

ITERS = 4
NR = 8
NZ, NX = 8, 4
NC = NZ * NX
B = 128
D = 256
ROWS = NR * B
CHUNK = 64
SHIFT = 20.0
TO_LOG2 = 2.0 / math.log(2.0)
INV_LN2 = 1.0 / math.log(2.0)


def log2(v):
    return jnp.log(v) * INV_LN2


def wait_bytes(ref, sem):
    pltpu.make_async_copy(ref, ref, sem).wait()


def lanes_to_vector(acc_ref, b):
    return jnp.sum(acc_ref[pl.ds(b * B, B), :].T, axis=0, keepdims=True)


def spread(vec):
    return jnp.broadcast_to(vec, (B, B)).T


def kernel(
    noise, data, out,
    tile, dfull, nfull, top, acc, vec, uwide, colw, colv, colc, colm,
    rsrc, rdst, xsrc, xdst, zsrc, zdst, wts, num, den, numr, denr,
    own_sem, nsem, dsend, drecv, rsem, xsem, zsem, fsem,
):
    r = lax.axis_index("rows")
    c = lax.axis_index("cols")
    z = c // NX
    x = lax.rem(c, NX)

    def row_peer(k):
        return (lax.rem(r + k, NR), c)

    def x_peer(k):
        return (r, z * NX + lax.rem(x + k, NX))

    def z_peer(k):
        return (r, lax.rem(z + k, NZ) * NX + x)

    barrier = pltpu.get_barrier_semaphore()
    peers = [row_peer(k) for k in range(1, NR)]
    peers += [x_peer(k) for k in range(1, NX)] + [z_peer(k) for k in range(1, NZ)]
    for peer in peers:
        pl.semaphore_signal(barrier, inc=1, device_id=peer, device_id_type=MESH)
    pl.semaphore_wait(barrier, len(peers))

    def remote(src, dst, send, recv, peer):
        return pltpu.make_async_remote_copy(
            src_ref=src, dst_ref=dst, send_sem=send, recv_sem=recv, device_id=peer, device_id_type=MESH
        )

    def pass_on(block, k):
        remote(dfull.at[block], dfull.at[block], dsend, drecv.at[block], z_peer(k)).start()

    def source(dz, dx):
        return lax.rem(z + dz + NZ, NZ) * NX + lax.rem(x + dx + NX, NX)

    own_d = pltpu.make_async_copy(data, dfull.at[c], own_sem.at[0])
    own_d.start()
    for k in (1, NZ - 1):
        remote(data, dfull.at[c], dsend, drecv.at[c], z_peer(k)).start()
    for k in range(1, NX):
        remote(data, dfull.at[c], dsend, drecv.at[c], x_peer(k)).start()
    own_n = pltpu.make_async_copy(noise, nfull.at[r], own_sem.at[1])
    own_n.start()
    for k in range(1, NR):
        remote(noise, nfull.at[r], nsem.at[0], nsem.at[1], row_peer(k)).start()

    top[...] = jnp.full_like(top, -1e30)
    acc[...] = jnp.zeros_like(acc)

    def add_set(dz):
        base = pl.multiple_of(lax.rem(z + dz + NZ, NZ) * NX, NX)
        right = dfull[pl.ds(base, NX)].reshape(NX * B, D)

        def rows_step(i, carry):
            left = nfull[pl.ds(2 * i, 2)].reshape(2 * B, D)
            s = lax.dot_general(left, right, (((1,), (1,)), ((), ())), preferred_element_type=F32)
            s = s * (D ** -0.5 * TO_LOG2)
            rows = pl.ds(pl.multiple_of(i * 2 * B, 2 * B), 2 * B)
            for j in range(NX):
                tile[base + j, rows, :] = s[:, j * B:(j + 1) * B]
            return carry

        lax.fori_loop(0, NR // 2, rows_step, 0)

        def lse_step(i, carry):
            rows = pl.ds(pl.multiple_of(i * CHUNK, CHUNK), CHUNK)
            s = [tile[base + j, rows, :] for j in range(NX)]
            old = top[rows, :]
            new = jnp.maximum(old, jnp.maximum(jnp.maximum(s[0], s[1]), jnp.maximum(s[2], s[3])))
            total = acc[rows, :] * jnp.exp2(old - new)
            for j in range(NX):
                total = total + jnp.exp2(s[j] - new)
            top[rows, :] = new
            acc[rows, :] = total
            return carry

        lax.fori_loop(0, ROWS // CHUNK, lse_step, 0)

    for dx in range(1, NX):
        block = source(0, -dx)
        wait_bytes(dfull.at[block], drecv.at[block])
        pass_on(block, 1)
        pass_on(block, NZ - 1)
    wait_bytes(nfull.at[pl.ds(0, NR - 1)], nsem.at[1])
    own_n.wait()
    own_d.wait()
    add_set(0)
    half = NZ // 2
    for s in range(1, half):
        for dx in range(NX):
            ahead, behind = source(-s, -dx), source(s, -dx)
            wait_bytes(dfull.at[ahead], drecv.at[ahead])
            if s < half - 1 or dx < NX // 2:
                pass_on(ahead, 1)
            wait_bytes(dfull.at[behind], drecv.at[behind])
            if s < half - 1 or dx >= NX // 2:
                pass_on(behind, NZ - 1)
        add_set(-s)
        add_set(s)
    for dx in range(NX):
        block = source(half, -dx)
        wait_bytes(dfull.at[block], drecv.at[block])
    add_set(half)
    wait_bytes(dfull.at[pl.ds(0, NC - 1)], dsend)
    wait_bytes(nfull.at[pl.ds(0, NR - 1)], nsem.at[0])

    def exchange(src, dst, sems, group, size):
        for k in range(1, size):
            remote(src, dst.at[k - 1], sems.at[0], sems.at[1], group(k)).start()
        wait_bytes(dst, sems.at[1])
        wait_bytes(dst, sems.at[0])

    def lse(own, others, n):
        high = own
        for k in range(n):
            high = jnp.maximum(high, others[k])
        total = jnp.exp2(own - high)
        for k in range(n):
            total = total + jnp.exp2(others[k] - high)
        return high + log2(total)

    def add(own, others, n):
        for k in range(n):
            own = own + others[k]
        return own

    def finish_rows(i, carry):
        rows = pl.ds(pl.multiple_of(i * CHUNK, CHUNK), CHUNK)
        high = top[rows, :]
        row_top = jnp.max(high, axis=1, keepdims=True)
        acc[rows, :] = acc[rows, :] * jnp.exp2(high - row_top)
        top[rows, :] = jnp.broadcast_to(row_top, (CHUNK, B))
        return carry

    lax.fori_loop(0, ROWS // CHUNK, finish_rows, 0)
    for b in range(NR):
        row_top = top[pl.ds(b * B, B), :].T[0:1, :]
        rsrc[0, b:b + 1, :] = row_top + log2(lanes_to_vector(acc, b))
    exchange(rsrc.at[0], rdst.at[0], rsem.at[0], row_peer, NR)
    vec[...] = -lse(rsrc[0], rdst.at[0], NR - 1)

    def widen():
        for b in range(NR):
            uwide[pl.ds(b * B, B), :] = spread(vec[b:b + 1, :])

    widen()

    def first_cols(j, carry):
        def top_step(i, high):
            rows = pl.ds(pl.multiple_of(i * 2 * B, 2 * B), 2 * B)
            zed = tile[j, rows, :] + uwide[rows, :]
            return jnp.maximum(high, jnp.max(zed.reshape(2 * B // 8, 8, B), axis=0))

        high = lax.fori_loop(0, ROWS // (2 * B), top_step, jnp.full((8, B), -1e30, F32))
        high = jnp.max(high, axis=0, keepdims=True)

        def exp_step(i, total):
            rows = pl.ds(pl.multiple_of(i * 2 * B, 2 * B), 2 * B)
            e = jnp.exp2(tile[j, rows, :] + uwide[rows, :] - (high - SHIFT))
            tile[j, rows, :] = e
            return total + jnp.sum(e.reshape(2 * B // 8, 8, B), axis=0)

        total = lax.fori_loop(0, ROWS // (2 * B), exp_step, jnp.zeros((8, B), F32))
        colm[pl.ds(j, 1), :] = high
        colc[pl.ds(j, 1), :] = jnp.sum(total, axis=0, keepdims=True)
        return carry

    lax.fori_loop(0, NC, first_cols, 0)
    xsrc[0] = colm[...] + (log2(colc[...]) - SHIFT)
    exchange(xsrc.at[0], xdst.at[0], xsem.at[0], x_peer, NX)
    zsrc[0] = lse(xsrc[0], xdst.at[0], NX - 1)
    exchange(zsrc.at[0], zdst.at[0], zsem.at[0], z_peer, NZ)
    colw[...] = jnp.exp2(colm[...] - lse(zsrc[0], zdst.at[0], NZ - 1) + SHIFT)
    colv[...] = colw[...]

    def iteration(t, carry):
        def rows_pass(i, carry):
            rows = pl.ds(pl.multiple_of(i * CHUNK, CHUNK), CHUNK)
            total = tile[0, rows, :] * colv[0:1, :]
            for j in range(1, NC):
                total = total + tile[j, rows, :] * colv[j:j + 1, :]
            acc[rows, :] = total
            return carry

        lax.fori_loop(0, ROWS // CHUNK, rows_pass, 0)
        for b in range(NR):
            rsrc[t, b:b + 1, :] = lanes_to_vector(acc, b)
        exchange(rsrc.at[t], rdst.at[t], rsem.at[t], row_peer, NR)
        vec[...] = 1.0 / add(rsrc[t], rdst.at[t], NR - 1)
        widen()

        def cols_pass(j, carry):
            def step(i, totals):
                rows = pl.ds(pl.multiple_of(i * 2 * B, 2 * B), 2 * B)
                u = uwide[rows, :]
                return tuple(
                    total + jnp.sum((tile[4 * j + k, rows, :] * u).reshape(2 * B // 8, 8, B), axis=0)
                    for k, total in enumerate(totals)
                )

            totals = lax.fori_loop(0, ROWS // (2 * B), step, (jnp.zeros((8, B), F32),) * 4)
            for k in range(4):
                colc[pl.ds(4 * j + k, 1), :] = jnp.sum(totals[k], axis=0, keepdims=True)
            return carry

        lax.fori_loop(0, NC // 4, cols_pass, 0)
        xsrc[t] = colc[...] * colw[...]
        exchange(xsrc.at[t], xdst.at[t], xsem.at[t], x_peer, NX)
        zsrc[t] = add(xsrc[t], xdst.at[t], NX - 1)
        exchange(zsrc.at[t], zdst.at[t], zsem.at[t], z_peer, NZ)
        colv[...] = colw[...] / add(zsrc[t], zdst.at[t], NZ - 1)
        return carry

    lax.fori_loop(1, ITERS, iteration, 0)

    def weigh(q):
        def step(i, carry):
            rows = pl.ds(pl.multiple_of(q * 2 * B + i * CHUNK, CHUNK), CHUNK)
            to = pl.ds(pl.multiple_of(i * CHUNK, CHUNK), CHUNK)
            total = jnp.zeros((CHUNK, B), F32)
            for j in range(NC):
                w = (tile[j, rows, :] * colv[j:j + 1, :]).astype(BF16)
                wts[to, j * B:(j + 1) * B] = w
                total = total + w.astype(F32)
            acc[to, :] = total
            return carry

        lax.fori_loop(0, 2 * B // CHUNK, step, 0)
        n = jnp.dot(wts[...], dfull[...].reshape(NC * B, D), preferred_element_type=F32)
        num[pl.ds(2 * q, 2)] = n.reshape(2, B, D)
        for b in range(2):
            den[2 * q + b] = lanes_to_vector(acc, b)

    def send(b):
        slot = lax.rem(r - b + NR, NR) - 1
        remote(num.at[b], numr.at[slot], fsem.at[0], fsem.at[1], (b, c)).start()
        remote(den.at[b], denr.at[slot], fsem.at[2], fsem.at[3], (b, c)).start()

    mine = r // 2

    def final(i, carry):
        q = lax.rem(mine + i, NR // 2)
        weigh(q)
        send(2 * q)
        send(2 * q + 1)
        return carry

    lax.fori_loop(1, NR // 2, final, 0)
    weigh(mine)
    send(2 * mine + 1 - lax.rem(r, 2))
    wait_bytes(numr, fsem.at[1])
    wait_bytes(denr, fsem.at[3])
    total = num[r]
    weight = den[r]
    for k in range(NR - 1):
        total = total + numr[k]
        weight = weight + denr[k]
    scale = spread(weight)
    out[:, 0:B] = total[:, 0:B] / scale
    out[:, B:D] = total[:, B:D] / scale
    wait_bytes(numr, fsem.at[0])
    wait_bytes(denr, fsem.at[2])


def solution(mesh):
    vmem, dma = pltpu.VMEM, pltpu.SemaphoreType.DMA
    scratch = [
        vmem((NC, ROWS, B), F32),
        vmem((NC, B, D), BF16),
        vmem((NR, B, D), BF16),
        vmem((ROWS, B), F32),
        vmem((ROWS, B), F32),
        vmem((NR, B), F32),
        vmem((ROWS, B), F32),
        vmem((NC, B), F32),
        vmem((NC, B), F32),
        vmem((NC, B), F32),
        vmem((NC, B), F32),
        vmem((ITERS, NR, B), F32),
        vmem((ITERS, NR - 1, NR, B), F32),
        vmem((ITERS, NC, B), F32),
        vmem((ITERS, NX - 1, NC, B), F32),
        vmem((ITERS, NC, B), F32),
        vmem((ITERS, NZ - 1, NC, B), F32),
        vmem((2 * B, NC * B), BF16),
        vmem((NR, B, D), F32),
        vmem((NR, 1, B), F32),
        vmem((NR - 1, B, D), F32),
        vmem((NR - 1, 1, B), F32),
        dma((2,)),
        dma((2,)),
        dma,
        dma((NC,)),
        dma((ITERS, 2)),
        dma((ITERS, 2)),
        dma((ITERS, 2)),
        dma((4,)),
    ]

    def per_device(noise, data):
        return pl.pallas_call(
            kernel,
            out_shape=jax.ShapeDtypeStruct((B, D), F32),
            in_specs=[pl.BlockSpec(memory_space=pltpu.VMEM)] * 2,
            out_specs=pl.BlockSpec(memory_space=pltpu.VMEM),
            scratch_shapes=scratch,
            compiler_params=pltpu.CompilerParams(
                collective_id=0, has_side_effects=True, vmem_limit_bytes=40 << 20
            ),
        )(noise, data)

    return jax.shard_map(
        per_device,
        mesh=mesh,
        in_specs=(P(("rows", "cols"), None), P(("cols", "rows"), None)),
        out_specs=P(("rows", "cols"), None),
        check_vma=False,
    )
```

```python
import functools
import math

import jax
import jax.numpy as jnp
from jax import lax
from jax.experimental import pallas as pl
from jax.experimental.pallas import tpu as pltpu
from jax.sharding import PartitionSpec as P

MESH = pl.DeviceIdType.MESH
F32 = jnp.float32
BF16 = jnp.bfloat16

ITERS = 4
NR = 8
NZ, NX = 8, 4
NC = NZ * NX
B = 128
D = 256
ROWS = NR * B
CHUNK = 64
SWEEP = 32
GROUP = 8
SHIFT = 20.0
TO_LOG2 = 2.0 / math.log(2.0)
INV_LN2 = 1.0 / math.log(2.0)


def log2(v):
    return jnp.log(v) * INV_LN2


def wait_bytes(ref, sem):
    pltpu.make_async_copy(ref, ref, sem).wait()


def lanes_to_vector(block):
    return jnp.sum(block.T, axis=0, keepdims=True)


def spread(vec):
    return jnp.broadcast_to(vec, (B, B)).T


def kernel(
    noise, data, out,
    tile, dfull, nfull, top, acc, vec, uwide, colw, colv, colc, colm, high8,
    rsrc, rdst, csrc, cmid, cdstx, cdstz, num, pair, numr,
    own_sem, nsem, dsend, drecv, rsem, csem, psem, fsem,
):
    r = lax.axis_index("rows")
    c = lax.axis_index("cols")
    z = c // NX
    x = lax.rem(c, NX)

    def row_peer(k):
        return (lax.rem(r + k, NR), c)

    def x_peer(k):
        return (r, z * NX + lax.rem(x + k, NX))

    def z_peer(k):
        return (r, lax.rem(z + k, NZ) * NX + x)

    barrier = pltpu.get_barrier_semaphore()
    peers = [row_peer(k) for k in range(1, NR)]
    peers += [x_peer(k) for k in range(1, NX)] + [z_peer(k) for k in range(1, NZ)]
    for peer in peers:
        pl.semaphore_signal(barrier, inc=1, device_id=peer, device_id_type=MESH)
    pl.semaphore_wait(barrier, len(peers))

    def remote(src, dst, send, recv, peer):
        return pltpu.make_async_remote_copy(
            src_ref=src, dst_ref=dst, send_sem=send, recv_sem=recv, device_id=peer, device_id_type=MESH
        )

    def pass_on(block, k):
        remote(dfull.at[block], dfull.at[block], dsend, drecv.at[block], z_peer(k)).start()

    def source(dz, dx):
        return lax.rem(z + dz + NZ, NZ) * NX + lax.rem(x + dx + NX, NX)

    own_d = pltpu.make_async_copy(data, dfull.at[c], own_sem.at[0])
    own_d.start()
    for k in (1, NZ - 1):
        remote(data, dfull.at[c], dsend, drecv.at[c], z_peer(k)).start()
    for k in range(1, NX):
        remote(data, dfull.at[c], dsend, drecv.at[c], x_peer(k)).start()
    own_n = pltpu.make_async_copy(noise, nfull.at[r], own_sem.at[1])
    own_n.start()
    for k in range(1, NR):
        remote(noise, nfull.at[r], nsem.at[0], nsem.at[1], row_peer(k)).start()

    top[...] = jnp.full_like(top, -1e30)
    acc[...] = jnp.zeros_like(acc)

    def add_set(dz):
        base = pl.multiple_of(lax.rem(z + dz + NZ, NZ) * NX, NX)
        right = dfull[pl.ds(base, NX)].reshape(NX * B, D)

        def rows_step(i, carry):
            left = nfull[pl.ds(2 * i, 2)].reshape(2 * B, D)
            s = lax.dot_general(left, right, (((1,), (1,)), ((), ())), preferred_element_type=F32)
            s = s * (D ** -0.5 * TO_LOG2)
            rows = pl.ds(pl.multiple_of(i * 2 * B, 2 * B), 2 * B)
            for j in range(NX):
                tile[base + j, rows, :] = s[:, j * B:(j + 1) * B]
            return carry

        lax.fori_loop(0, NR // 2, rows_step, 0)

        def lse_step(i, carry):
            rows = pl.ds(pl.multiple_of(i * CHUNK, CHUNK), CHUNK)
            s = [tile[base + j, rows, :] for j in range(NX)]
            old = top[rows, :]
            new = jnp.maximum(old, jnp.maximum(jnp.maximum(s[0], s[1]), jnp.maximum(s[2], s[3])))
            total = acc[rows, :] * jnp.exp2(old - new)
            for j in range(NX):
                total = total + jnp.exp2(s[j] - new)
            top[rows, :] = new
            acc[rows, :] = total
            return carry

        lax.fori_loop(0, ROWS // CHUNK, lse_step, 0)

    for dx in range(1, NX):
        block = source(0, -dx)
        wait_bytes(dfull.at[block], drecv.at[block])
        pass_on(block, 1)
        pass_on(block, NZ - 1)
    wait_bytes(nfull.at[pl.ds(0, NR - 1)], nsem.at[1])
    own_n.wait()
    own_d.wait()
    add_set(0)
    half = NZ // 2
    for s in range(1, half):
        for dx in range(NX):
            ahead, behind = source(-s, -dx), source(s, -dx)
            wait_bytes(dfull.at[ahead], drecv.at[ahead])
            if s < half - 1 or dx < NX // 2:
                pass_on(ahead, 1)
            wait_bytes(dfull.at[behind], drecv.at[behind])
            if s < half - 1 or dx >= NX // 2:
                pass_on(behind, NZ - 1)
        add_set(-s)
        add_set(s)
    for dx in range(NX):
        block = source(half, -dx)
        wait_bytes(dfull.at[block], drecv.at[block])
    add_set(half)
    wait_bytes(dfull.at[pl.ds(0, NC - 1)], dsend)
    wait_bytes(nfull.at[pl.ds(0, NR - 1)], nsem.at[0])

    def send_all(src, dst, sems, group, size):
        for k in range(1, size):
            remote(src, dst.at[k - 1], sems.at[0], sems.at[1], group(k)).start()

    def lse(own, others, n):
        high = own
        for k in range(n):
            high = jnp.maximum(high, others[k])
        total = jnp.exp2(own - high)
        for k in range(n):
            total = total + jnp.exp2(others[k] - high)
        return high + log2(total)

    def add(own, others, n):
        for k in range(n):
            own = own + others[k]
        return own

    def over_rows(t, combine):
        dst = rdst.at[t]
        send_all(rsrc.at[t], dst, rsem.at[t], row_peer, NR)
        wait_bytes(dst, rsem.at[t, 1])
        wait_bytes(dst, rsem.at[t, 0])
        return combine(rsrc[t], dst, NR - 1)

    def over_cols(t, combine):
        send_all(csrc.at[t, 1], cdstz.at[t, 0], csem.at[t, 1], z_peer, NZ)
        send_all(csrc.at[t, 0], cdstx.at[t, 0], csem.at[t, 0], x_peer, NX)
        wait_bytes(cdstx.at[t, 0], csem.at[t, 0, 1])
        cmid[t, 0] = combine(csrc[t, 0], cdstx.at[t, 0], NX - 1)
        send_all(cmid.at[t, 0], cdstz.at[t, 1], csem.at[t, 2], z_peer, NZ)
        wait_bytes(cdstz.at[t, 0], csem.at[t, 1, 1])
        cmid[t, 1] = combine(csrc[t, 1], cdstz.at[t, 0], NZ - 1)
        send_all(cmid.at[t, 1], cdstx.at[t, 1], csem.at[t, 3], x_peer, NX)
        wait_bytes(cdstz.at[t, 1], csem.at[t, 2, 1])
        first = combine(cmid[t, 0], cdstz.at[t, 1], NZ - 1)
        wait_bytes(cdstx.at[t, 1], csem.at[t, 3, 1])
        second = combine(cmid[t, 1], cdstx.at[t, 1], NX - 1)
        wait_bytes(cdstx.at[t, 0], csem.at[t, 0, 0])
        wait_bytes(cdstz.at[t, 0], csem.at[t, 1, 0])
        wait_bytes(cdstz.at[t, 1], csem.at[t, 2, 0])
        wait_bytes(cdstx.at[t, 1], csem.at[t, 3, 0])
        return first, second

    for b in range(NR):
        rows = pl.ds(b * B, B)
        high = top[rows, :].T
        row_top = jnp.max(high, axis=0, keepdims=True)
        total = jnp.sum(acc[rows, :].T * jnp.exp2(high - row_top), axis=0, keepdims=True)
        rsrc[0, b:b + 1, :] = row_top + log2(total)
    vec[...] = -over_rows(0, lse)

    def widen():
        for b in range(NR):
            uwide[pl.ds(b * B, B), :] = spread(vec[b:b + 1, :])

    widen()

    fold = (SWEEP // 8, 8, B)
    zeros = (jnp.zeros((8, B), F32),) * NC

    def top_step(i, highs):
        rows = pl.ds(pl.multiple_of(i * SWEEP, SWEEP), SWEEP)
        u = uwide[rows, :]
        return tuple(
            jnp.maximum(high, jnp.max((tile[j, rows, :] + u).reshape(fold), axis=0)) for j, high in enumerate(highs)
        )

    highs = lax.fori_loop(0, ROWS // SWEEP, top_step, (jnp.full((8, B), -1e30, F32),) * NC)
    for j in range(NC):
        high = jnp.max(highs[j], axis=0, keepdims=True)
        colm[j:j + 1, :] = high
        high8[j] = jnp.broadcast_to(high - SHIFT, (8, B))

    def exp_step(i, totals):
        rows = pl.ds(pl.multiple_of(i * SWEEP, SWEEP), SWEEP)
        u = uwide[rows, :].reshape(fold)
        sums = []
        for j in range(NC):
            e = jnp.exp2(tile[j, rows, :].reshape(fold) + (u - high8[j]))
            tile[j, rows, :] = e.reshape(SWEEP, B)
            sums.append(totals[j] + jnp.sum(e, axis=0))
        return tuple(sums)

    totals = lax.fori_loop(0, ROWS // SWEEP, exp_step, zeros)
    for j in range(NC):
        colc[j:j + 1, :] = jnp.sum(totals[j], axis=0, keepdims=True)
    hc = NC // 2
    csrc[0] = (colm[...] + (log2(colc[...]) - SHIFT)).reshape(2, hc, B)
    for h, logs in enumerate(over_cols(0, lse)):
        half = pl.ds(h * hc, hc)
        colw[half, :] = jnp.exp2(colm[half, :] - logs + SHIFT)
        colv[half, :] = colw[half, :]

    def iteration(t, carry):
        def rows_pass(i, carry):
            rows = pl.ds(pl.multiple_of(i * 2 * B, 2 * B), 2 * B)
            total = tile[0, rows, :] * colv[0:1, :]
            for j in range(1, NC):
                total = total + tile[j, rows, :] * colv[j:j + 1, :]
            acc[rows, :] = total
            return carry

        lax.fori_loop(0, ROWS // (2 * B), rows_pass, 0)
        for b in range(NR):
            rsrc[t, b:b + 1, :] = lanes_to_vector(acc[pl.ds(b * B, B), :])
        vec[...] = 1.0 / over_rows(t, add)
        widen()

        def step(i, totals):
            rows = pl.ds(pl.multiple_of(i * SWEEP, SWEEP), SWEEP)
            u = uwide[rows, :]
            return tuple(
                total + jnp.sum((tile[j, rows, :] * u).reshape(fold), axis=0) for j, total in enumerate(totals)
            )

        totals = lax.fori_loop(0, ROWS // SWEEP, step, zeros)
        for j in range(NC):
            colc[j:j + 1, :] = jnp.sum(totals[j], axis=0, keepdims=True)
        csrc[t] = (colc[...] * colw[...]).reshape(2, hc, B)
        for h, sums in enumerate(over_cols(t, add)):
            half = pl.ds(h * hc, hc)
            colv[half, :] = colw[half, :] / sums
        return carry

    lax.fori_loop(1, ITERS, iteration, 0)

    y = r // 2
    core = lax.rem(r, 2)
    partner = (2 * y + 1 - core, c)

    def weigh(i):
        q = lax.rem(y + i + 1, NR // 2)
        rows = pl.ds(pl.multiple_of(q * 2 * B, 2 * B), 2 * B)
        n = total = None
        for g in range(0, NC, GROUP):
            parts = []
            for j in range(g, g + GROUP):
                w = (tile[j, rows, :] * colv[j:j + 1, :]).astype(BF16)
                parts.append(w)
                wide = w.astype(F32)
                total = wide if total is None else total + wide
            part = jnp.dot(
                jnp.concatenate(parts, axis=1),
                dfull[pl.ds(g, GROUP)].reshape(GROUP * B, D),
                preferred_element_type=F32,
            )
            n = part if n is None else n + part
        for h in range(2):
            num[i, h, 0:B] = n[h * B:(h + 1) * B]
            sums = lanes_to_vector(total[h * B:(h + 1) * B])
            num[i, h, B:B + 8, 0:B] = jnp.broadcast_to(sums, (8, B))
            num[i, h, B:B + 8, B:D] = jnp.zeros((8, B), F32)
        remote(num.at[i, 1 - core], pair.at[i], psem.at[0, i], psem.at[1, i], partner).start()

    def join(i):
        wait_bytes(pair.at[i], psem.at[1, i])
        num[i, core] = num[i, core] + pair[i]

    def hand_over(i):
        join(i)
        q = lax.rem(y + i + 1, NR // 2)
        remote(num.at[i, core], numr.at[i], fsem.at[0], fsem.at[1], (2 * q + core, c)).start()

    weigh(0)

    def final(i, carry):
        weigh(i)
        hand_over(i - 1)
        return carry

    last = NR // 2 - 1
    lax.fori_loop(1, last + 1, final, 0)
    join(last)
    wait_bytes(numr, fsem.at[1])
    total = num[last, core]
    for k in range(last):
        total = total + numr[k]
    scale = spread(total[B:B + 1, 0:B])
    out[:, 0:B] = total[0:B, 0:B] / scale
    out[:, B:D] = total[0:B, B:D] / scale
    wait_bytes(numr, fsem.at[0])
    for i in range(last + 1):
        wait_bytes(pair.at[i], psem.at[0, i])


def solution(mesh):
    vmem, dma = pltpu.VMEM, pltpu.SemaphoreType.DMA
    scratch = [
        vmem((NC, ROWS, B), F32),
        vmem((NC, B, D), BF16),
        vmem((NR, B, D), BF16),
        vmem((ROWS, B), F32),
        vmem((ROWS, B), F32),
        vmem((NR, B), F32),
        vmem((ROWS, B), F32),
        vmem((NC, B), F32),
        vmem((NC, B), F32),
        vmem((NC, B), F32),
        vmem((NC, B), F32),
        vmem((NC, 8, B), F32),
        vmem((ITERS, NR, B), F32),
        vmem((ITERS, NR - 1, NR, B), F32),
        vmem((ITERS, 2, NC // 2, B), F32),
        vmem((ITERS, 2, NC // 2, B), F32),
        vmem((ITERS, 2, NX - 1, NC // 2, B), F32),
        vmem((ITERS, 2, NZ - 1, NC // 2, B), F32),
        vmem((NR // 2, 2, B + 8, D), F32),
        vmem((NR // 2, B + 8, D), F32),
        vmem((NR // 2 - 1, B + 8, D), F32),
        dma((2,)),
        dma((2,)),
        dma,
        dma((NC,)),
        dma((ITERS, 2)),
        dma((ITERS, 4, 2)),
        dma((2, NR // 2)),
        dma((2,)),
    ]

    def per_device(noise, data):
        return pl.pallas_call(
            kernel,
            out_shape=jax.ShapeDtypeStruct((B, D), F32),
            in_specs=[pl.BlockSpec(memory_space=pltpu.VMEM)] * 2,
            out_specs=pl.BlockSpec(memory_space=pltpu.VMEM),
            scratch_shapes=scratch,
            compiler_params=pltpu.CompilerParams(
                collective_id=0, has_side_effects=True, vmem_limit_bytes=40 << 20
            ),
        )(noise, data)

    return jax.shard_map(
        per_device,
        mesh=mesh,
        in_specs=(P(("rows", "cols"), None), P(("cols", "rows"), None)),
        out_specs=P(("rows", "cols"), None),
        check_vma=False,
    )
```

```python
import functools
import math

import jax
import jax.numpy as jnp
from jax import lax
from jax.experimental import pallas as pl
from jax.experimental.pallas import tpu as pltpu
from jax.sharding import PartitionSpec as P

MESH = pl.DeviceIdType.MESH
F32 = jnp.float32
BF16 = jnp.bfloat16

ITERS = 4
NR = 8
NZ, NX = 8, 4
NC = NZ * NX
B = 128
D = 256
HALF = B // 2
ROWS = NR * B
CHUNK = 64
SWEEP = 32
GROUP = 8
SHIFT = 20.0
TO_LOG2 = 2.0 / math.log(2.0)
INV_LN2 = 1.0 / math.log(2.0)


def log2(v):
    return jnp.log(v) * INV_LN2


def wait_bytes(ref, sem):
    pltpu.make_async_copy(ref, ref, sem).wait()


def lanes_to_vector(block):
    return jnp.sum(block.T, axis=0, keepdims=True)


def spread(vec):
    return jnp.broadcast_to(vec, (B, B)).T


def kernel(
    noise, data, out,
    tile, dfull, nfull, top, acc, vec, uwide, colw, colv, colc, colm, high8,
    rsrc, rdst, csrc, cmid, cdstx, cdstz, num, pair, numr,
    own_sem, nsem, dsend, drecv, rsem, csem, psem, fsem,
):
    r = lax.axis_index("rows")
    c = lax.axis_index("cols")
    z = c // NX
    x = lax.rem(c, NX)

    def row_peer(k):
        return (lax.rem(r + k, NR), c)

    def x_peer(k):
        return (r, z * NX + lax.rem(x + k, NX))

    def z_peer(k):
        return (r, lax.rem(z + k, NZ) * NX + x)

    own_d = pltpu.make_async_copy(data, dfull.at[c], own_sem.at[0])
    own_d.start()
    own_n = pltpu.make_async_copy(noise, nfull.at[r], own_sem.at[1])
    own_n.start()
    top[...] = jnp.full_like(top, -1e30)
    acc[...] = jnp.zeros_like(acc)

    barrier = pltpu.get_barrier_semaphore()
    peers = [row_peer(k) for k in range(1, NR)]
    peers += [x_peer(k) for k in range(1, NX)] + [z_peer(k) for k in range(1, NZ)]
    for peer in peers:
        pl.semaphore_signal(barrier, inc=1, device_id=peer, device_id_type=MESH)
    own_d.wait()
    own_n.wait()
    pl.semaphore_wait(barrier, len(peers))

    def remote(src, dst, send, recv, peer):
        return pltpu.make_async_remote_copy(
            src_ref=src, dst_ref=dst, send_sem=send, recv_sem=recv, device_id=peer, device_id_type=MESH
        )

    def part(block, h):
        return dfull.at[block, pl.ds(h * HALF, HALF)]

    def give(block, h, peer):
        remote(part(block, h), part(block, h), dsend, drecv.at[h, block], peer).start()

    def take(block, h):
        wait_bytes(part(block, h), drecv.at[h, block])

    def source(dz, dx):
        return lax.rem(z + dz + NZ, NZ) * NX + lax.rem(x + dx + NX, NX)

    def across(block):
        for k in range(1, NX):
            give(block, 1, x_peer(k))

    for h in (0, 1):
        for k in (1, NZ - 1):
            give(c, 1 - h, z_peer(k))
        for k in range(1, NX):
            give(c, h, x_peer(k))
    for k in range(1, NR):
        remote(nfull.at[r], nfull.at[r], nsem.at[0], nsem.at[1], row_peer(k)).start()

    def scores(dz, i):
        base = pl.multiple_of(lax.rem(z + dz + NZ, NZ) * NX, NX)
        right = dfull[pl.ds(base, NX)].reshape(NX * B, D)
        left = nfull[pl.ds(2 * i, 2)].reshape(2 * B, D)
        s = lax.dot_general(left, right, (((1,), (1,)), ((), ())), preferred_element_type=F32)
        s = s * (D ** -0.5 * TO_LOG2)
        for k in range(0, 2 * B, CHUNK):
            rows = pl.ds(i * 2 * B + k, CHUNK)
            part = [s[k:k + CHUNK, j * B:(j + 1) * B] for j in range(NX)]
            for j in range(NX):
                tile[base + j, rows, :] = part[j]
            old = top[rows, :]
            new = jnp.maximum(old, jnp.maximum(jnp.maximum(part[0], part[1]), jnp.maximum(part[2], part[3])))
            total = acc[rows, :] * jnp.exp2(old - new)
            for j in range(NX):
                total = total + jnp.exp2(part[j] - new)
            top[rows, :] = new
            acc[rows, :] = total

    ready = []

    def work(count):
        for _ in range(min(count, len(ready))):
            ready.pop(0)()

    def add_set(dz):
        def rest():
            for dx in range(1, NX):
                take(source(dz, -dx), 1)
            scores(dz, 0)

        ready.append(rest)
        for i in range(1, NR // 2):
            ready.append(functools.partial(scores, dz, i))

    for dx in range(1, NX):
        block = source(0, -dx)
        take(block, 0)
        give(block, 0, z_peer(1))
        give(block, 0, z_peer(NZ - 1))
    wait_bytes(nfull.at[pl.ds(0, NR - 1)], nsem.at[1])
    add_set(0)
    half = NZ // 2
    for s in range(1, half):
        onward = s < half - 1
        ahead, behind = source(-s, 0), source(s, 0)
        take(ahead, 1)
        across(ahead)
        if onward:
            give(ahead, 1, z_peer(1))
        work(1)
        take(behind, 1)
        give(behind, 1, z_peer(NZ - 1))
        across(behind)
        work(1)
        for dx in range(NX):
            ahead, behind = source(-s, -dx), source(s, -dx)
            take(ahead, 0)
            if onward or dx != 2:
                give(ahead, 0, z_peer(1))
            work(1)
            take(behind, 0)
            if onward or dx == 2:
                give(behind, 0, z_peer(NZ - 1))
            work(1)
        add_set(-s)
        add_set(s)
    take(source(half, 0), 1)
    across(source(half, 0))
    work(2)
    for dx in range(NX):
        take(source(half, -dx), 0)
        work(1)
    add_set(half)
    work(len(ready))
    wait_bytes(dfull.at[pl.ds(0, NC - 1)], dsend)
    wait_bytes(nfull.at[pl.ds(0, NR - 1)], nsem.at[0])

    def send_all(src, dst, sems, group, size):
        for k in range(1, size):
            remote(src, dst.at[k - 1], sems.at[0], sems.at[1], group(k)).start()

    def lse(own, others, n):
        high = own
        for k in range(n):
            high = jnp.maximum(high, others[k])
        total = jnp.exp2(own - high)
        for k in range(n):
            total = total + jnp.exp2(others[k] - high)
        return high + log2(total)

    def add(own, others, n):
        for k in range(n):
            own = own + others[k]
        return own

    def over_rows(t, combine):
        dst = rdst.at[t]
        send_all(rsrc.at[t], dst, rsem.at[t], row_peer, NR)
        wait_bytes(dst, rsem.at[t, 1])
        wait_bytes(dst, rsem.at[t, 0])
        return combine(rsrc[t], dst, NR - 1)

    def over_cols(t, combine):
        send_all(csrc.at[t, 1], cdstz.at[t, 0], csem.at[t, 1], z_peer, NZ)
        send_all(csrc.at[t, 0], cdstx.at[t, 0], csem.at[t, 0], x_peer, NX)
        wait_bytes(cdstx.at[t, 0], csem.at[t, 0, 1])
        cmid[t, 0] = combine(csrc[t, 0], cdstx.at[t, 0], NX - 1)
        send_all(cmid.at[t, 0], cdstz.at[t, 1], csem.at[t, 2], z_peer, NZ)
        wait_bytes(cdstz.at[t, 0], csem.at[t, 1, 1])
        cmid[t, 1] = combine(csrc[t, 1], cdstz.at[t, 0], NZ - 1)
        send_all(cmid.at[t, 1], cdstx.at[t, 1], csem.at[t, 3], x_peer, NX)
        wait_bytes(cdstz.at[t, 1], csem.at[t, 2, 1])
        first = combine(cmid[t, 0], cdstz.at[t, 1], NZ - 1)
        wait_bytes(cdstx.at[t, 1], csem.at[t, 3, 1])
        second = combine(cmid[t, 1], cdstx.at[t, 1], NX - 1)
        wait_bytes(cdstx.at[t, 0], csem.at[t, 0, 0])
        wait_bytes(cdstz.at[t, 0], csem.at[t, 1, 0])
        wait_bytes(cdstz.at[t, 1], csem.at[t, 2, 0])
        wait_bytes(cdstx.at[t, 1], csem.at[t, 3, 0])
        return first, second

    for b in range(NR):
        rows = pl.ds(b * B, B)
        high = top[rows, :].T
        row_top = jnp.max(high, axis=0, keepdims=True)
        total = jnp.sum(acc[rows, :].T * jnp.exp2(high - row_top), axis=0, keepdims=True)
        rsrc[0, b:b + 1, :] = row_top + log2(total)
    vec[...] = -over_rows(0, lse)

    def widen():
        for b in range(NR):
            uwide[pl.ds(b * B, B), :] = spread(vec[b:b + 1, :])

    widen()

    fold = (SWEEP // 8, 8, B)
    zeros = (jnp.zeros((8, B), F32),) * NC

    def top_step(i, highs):
        rows = pl.ds(pl.multiple_of(i * SWEEP, SWEEP), SWEEP)
        u = uwide[rows, :]
        return tuple(
            jnp.maximum(high, jnp.max((tile[j, rows, :] + u).reshape(fold), axis=0)) for j, high in enumerate(highs)
        )

    highs = lax.fori_loop(0, ROWS // SWEEP, top_step, (jnp.full((8, B), -1e30, F32),) * NC)
    for j in range(NC):
        high = jnp.max(highs[j], axis=0, keepdims=True)
        colm[j:j + 1, :] = high
        high8[j] = jnp.broadcast_to(high - SHIFT, (8, B))

    def exp_step(i, totals):
        rows = pl.ds(pl.multiple_of(i * SWEEP, SWEEP), SWEEP)
        u = uwide[rows, :].reshape(fold)
        sums = []
        for j in range(NC):
            e = jnp.exp2(tile[j, rows, :].reshape(fold) + (u - high8[j]))
            tile[j, rows, :] = e.reshape(SWEEP, B)
            sums.append(totals[j] + jnp.sum(e, axis=0))
        return tuple(sums)

    totals = lax.fori_loop(0, ROWS // SWEEP, exp_step, zeros)
    for j in range(NC):
        colc[j:j + 1, :] = jnp.sum(totals[j], axis=0, keepdims=True)
    hc = NC // 2
    csrc[0] = (colm[...] + (log2(colc[...]) - SHIFT)).reshape(2, hc, B)
    for h, logs in enumerate(over_cols(0, lse)):
        half = pl.ds(h * hc, hc)
        colw[half, :] = jnp.exp2(colm[half, :] - logs + SHIFT)
        colv[half, :] = colw[half, :]

    def iteration(t, carry):
        def rows_pass(i, carry):
            rows = pl.ds(pl.multiple_of(i * 2 * B, 2 * B), 2 * B)
            total = tile[0, rows, :] * colv[0:1, :]
            for j in range(1, NC):
                total = total + tile[j, rows, :] * colv[j:j + 1, :]
            acc[rows, :] = total
            return carry

        lax.fori_loop(0, ROWS // (2 * B), rows_pass, 0)
        for b in range(NR):
            rsrc[t, b:b + 1, :] = lanes_to_vector(acc[pl.ds(b * B, B), :])
        vec[...] = 1.0 / over_rows(t, add)
        widen()

        def step(i, totals):
            rows = pl.ds(pl.multiple_of(i * SWEEP, SWEEP), SWEEP)
            u = uwide[rows, :]
            return tuple(
                total + jnp.sum((tile[j, rows, :] * u).reshape(fold), axis=0) for j, total in enumerate(totals)
            )

        totals = lax.fori_loop(0, ROWS // SWEEP, step, zeros)
        for j in range(NC):
            colc[j:j + 1, :] = jnp.sum(totals[j], axis=0, keepdims=True)
        csrc[t] = (colc[...] * colw[...]).reshape(2, hc, B)
        for h, sums in enumerate(over_cols(t, add)):
            half = pl.ds(h * hc, hc)
            colv[half, :] = colw[half, :] / sums
        return carry

    lax.fori_loop(1, ITERS, iteration, 0)

    y = r // 2
    core = lax.rem(r, 2)
    partner = (2 * y + 1 - core, c)

    def weigh(i):
        q = lax.rem(y + i + 1, NR // 2)
        rows = pl.ds(pl.multiple_of(q * 2 * B, 2 * B), 2 * B)
        n = total = None
        for g in range(0, NC, GROUP):
            parts = []
            for j in range(g, g + GROUP):
                w = (tile[j, rows, :] * colv[j:j + 1, :]).astype(BF16)
                parts.append(w)
                wide = w.astype(F32)
                total = wide if total is None else total + wide
            part = jnp.dot(
                jnp.concatenate(parts, axis=1),
                dfull[pl.ds(g, GROUP)].reshape(GROUP * B, D),
                preferred_element_type=F32,
            )
            n = part if n is None else n + part
        for h in range(2):
            num[i, h, 0:B] = n[h * B:(h + 1) * B]
            sums = lanes_to_vector(total[h * B:(h + 1) * B])
            num[i, h, B:B + 8, 0:B] = jnp.broadcast_to(sums, (8, B))
            num[i, h, B:B + 8, B:D] = jnp.zeros((8, B), F32)
        remote(num.at[i, 1 - core], pair.at[i], psem.at[0, i], psem.at[1, i], partner).start()

    def join(i):
        wait_bytes(pair.at[i], psem.at[1, i])
        num[i, core] = num[i, core] + pair[i]

    def hand_over(i):
        join(i)
        q = lax.rem(y + i + 1, NR // 2)
        remote(num.at[i, core], numr.at[i], fsem.at[0], fsem.at[1], (2 * q + core, c)).start()

    weigh(0)

    def final(i, carry):
        weigh(i)
        hand_over(i - 1)
        return carry

    last = NR // 2 - 1
    lax.fori_loop(1, last + 1, final, 0)
    join(last)
    wait_bytes(numr, fsem.at[1])
    total = num[last, core]
    for k in range(last):
        total = total + numr[k]
    scale = spread(total[B:B + 1, 0:B])
    out[:, 0:B] = total[0:B, 0:B] / scale
    out[:, B:D] = total[0:B, B:D] / scale
    wait_bytes(numr, fsem.at[0])
    for i in range(last + 1):
        wait_bytes(pair.at[i], psem.at[0, i])


def solution(mesh):
    vmem, dma = pltpu.VMEM, pltpu.SemaphoreType.DMA
    scratch = [
        vmem((NC, ROWS, B), F32),
        vmem((NC, B, D), BF16),
        vmem((NR, B, D), BF16),
        vmem((ROWS, B), F32),
        vmem((ROWS, B), F32),
        vmem((NR, B), F32),
        vmem((ROWS, B), F32),
        vmem((NC, B), F32),
        vmem((NC, B), F32),
        vmem((NC, B), F32),
        vmem((NC, B), F32),
        vmem((NC, 8, B), F32),
        vmem((ITERS, NR, B), F32),
        vmem((ITERS, NR - 1, NR, B), F32),
        vmem((ITERS, 2, NC // 2, B), F32),
        vmem((ITERS, 2, NC // 2, B), F32),
        vmem((ITERS, 2, NX - 1, NC // 2, B), F32),
        vmem((ITERS, 2, NZ - 1, NC // 2, B), F32),
        vmem((NR // 2, 2, B + 8, D), F32),
        vmem((NR // 2, B + 8, D), F32),
        vmem((NR // 2 - 1, B + 8, D), F32),
        dma((2,)),
        dma((2,)),
        dma,
        dma((2, NC)),
        dma((ITERS, 2)),
        dma((ITERS, 4, 2)),
        dma((2, NR // 2)),
        dma((2,)),
    ]

    def per_device(noise, data):
        return pl.pallas_call(
            kernel,
            out_shape=jax.ShapeDtypeStruct((B, D), F32),
            in_specs=[pl.BlockSpec(memory_space=pl.ANY)] * 2,
            out_specs=pl.BlockSpec(memory_space=pltpu.VMEM),
            scratch_shapes=scratch,
            compiler_params=pltpu.CompilerParams(
                collective_id=0, has_side_effects=True, vmem_limit_bytes=40 << 20
            ),
        )(noise, data)

    return jax.shard_map(
        per_device,
        mesh=mesh,
        in_specs=(P(("rows", "cols"), None), P(("cols", "rows"), None)),
        out_specs=P(("rows", "cols"), None),
        check_vma=False,
    )
```

```python
import functools
import math

import jax
import jax.numpy as jnp
from jax import lax
from jax.experimental import pallas as pl
from jax.experimental.pallas import tpu as pltpu
from jax.sharding import PartitionSpec as P

MESH = pl.DeviceIdType.MESH
F32 = jnp.float32
BF16 = jnp.bfloat16

ITERS = 4
NR = 8
NZ, NX = 8, 4
NC = NZ * NX
B = 128
D = 256
SPLIT = 48
ROWS = NR * B
CHUNK = 64
SWEEP = 32
GROUP = 8
SHIFT = 20.0
TO_LOG2 = 2.0 / math.log(2.0)
INV_LN2 = 1.0 / math.log(2.0)


def log2(v):
    return jnp.log(v) * INV_LN2


def wait_bytes(ref, sem):
    pltpu.make_async_copy(ref, ref, sem).wait()


def lanes_to_vector(block):
    return jnp.sum(block.T, axis=0, keepdims=True)


def spread(vec):
    return jnp.broadcast_to(vec, (B, B)).T


def kernel(
    noise, data, out,
    tile, dfull, nfull, top, acc, uwide, colw, colv, colc, colm, high8,
    rsrc, rdst, csrc, cmid, cdstx, cdstz, num, pair, numr,
    own_sem, nsem, dsend, drecv, rsem, csem, psem, fsem,
):
    r = lax.axis_index("rows")
    c = lax.axis_index("cols")
    z = c // NX
    x = lax.rem(c, NX)

    def row_peer(k):
        return (lax.rem(r + k, NR), c)

    def x_peer(k):
        return (r, z * NX + lax.rem(x + k, NX))

    def z_peer(k):
        return (r, lax.rem(z + k, NZ) * NX + x)

    own_d = pltpu.make_async_copy(data, dfull.at[c], own_sem.at[0])
    own_d.start()
    own_n = pltpu.make_async_copy(noise, nfull.at[r], own_sem.at[1])
    own_n.start()
    top[...] = jnp.full_like(top, -1e30)
    acc[...] = jnp.zeros_like(acc)

    barrier = pltpu.get_barrier_semaphore()
    peers = [row_peer(k) for k in range(1, NR)]
    peers += [x_peer(k) for k in range(1, NX)] + [z_peer(k) for k in range(1, NZ)]
    for peer in peers:
        pl.semaphore_signal(barrier, inc=1, device_id=peer, device_id_type=MESH)
    own_d.wait()
    own_n.wait()
    pl.semaphore_wait(barrier, len(peers))

    def remote(src, dst, send, recv, peer):
        return pltpu.make_async_remote_copy(
            src_ref=src, dst_ref=dst, send_sem=send, recv_sem=recv, device_id=peer, device_id_type=MESH
        )

    def part(block, h):
        return dfull.at[block, pl.ds(h * SPLIT, SPLIT + h * (B - 2 * SPLIT))]

    def give(block, h, peer):
        remote(part(block, h), part(block, h), dsend, drecv.at[h, block], peer).start()

    def take(block, h):
        wait_bytes(part(block, h), drecv.at[h, block])

    def source(dz, dx):
        return lax.rem(z + dz + NZ, NZ) * NX + lax.rem(x + dx + NX, NX)

    def across(block):
        for k in range(1, NX):
            give(block, 1, x_peer(k))

    for h in (0, 1):
        for k in range(1, NX):
            give(c, h, x_peer(k))
        for k in (2, NZ - 2, 1, NZ - 1):
            give(c, 1 - h, z_peer(k))
    for k in range(1, NR):
        remote(nfull.at[r], nfull.at[r], nsem.at[0], nsem.at[1], row_peer(k)).start()

    def scores(dz, i):
        base = pl.multiple_of(lax.rem(z + dz + NZ, NZ) * NX, NX)
        right = dfull[pl.ds(base, NX)].reshape(NX * B, D)
        left = nfull[pl.ds(2 * i, 2)].reshape(2 * B, D)
        s = lax.dot_general(left, right, (((1,), (1,)), ((), ())), preferred_element_type=F32)
        s = s * (D ** -0.5 * TO_LOG2)
        for k in range(0, 2 * B, CHUNK):
            rows = pl.ds(i * 2 * B + k, CHUNK)
            part = [s[k:k + CHUNK, j * B:(j + 1) * B] for j in range(NX)]
            for j in range(NX):
                tile[base + j, rows, :] = part[j]
            old = top[rows, :]
            new = jnp.maximum(old, jnp.maximum(jnp.maximum(part[0], part[1]), jnp.maximum(part[2], part[3])))
            total = acc[rows, :] * jnp.exp2(old - new)
            for j in range(NX):
                total = total + jnp.exp2(part[j] - new)
            top[rows, :] = new
            acc[rows, :] = total

    ready = []

    def work(count):
        for _ in range(min(count, len(ready))):
            ready.pop(0)()

    def add_set(dz):
        def rest():
            for dx in range(1, NX):
                take(source(dz, -dx), 1)
            scores(dz, 0)

        ready.append(rest)
        for i in range(1, NR // 2):
            ready.append(functools.partial(scores, dz, i))

    half = NZ // 2
    others = (1, 3, 2)

    def far(h, turn):
        for sign in (-1, 1):
            block = source(2 * sign, 0)
            take(block, h)
            if sign == turn:
                give(block, h, z_peer((NZ - 2 * sign) % NZ))
            give(block, h, z_peer((NZ - sign) % NZ))
            if h:
                across(block)

    def along(d):
        for dx in others:
            for sign in (-1, 1):
                block = source(d * sign, -dx)
                take(block, 0)
                if d < half - 1 or (dx != 2) == (sign < 0):
                    give(block, 0, z_peer((NZ - sign) % NZ))
                work(1)

    def spread_second(d):
        for sign in (-1, 1)[:2 if d < half else 1]:
            block = source(d * sign, 0)
            take(block, 1)
            across(block)
            work(1)

    for dx in others:
        block = source(0, -dx)
        take(block, 0)
        give(block, 0, z_peer(1))
        give(block, 0, z_peer(NZ - 1))
    spread_second(1)
    far(1, 1)
    far(0, -1)
    along(1)
    wait_bytes(nfull.at[pl.ds(0, NR - 1)], nsem.at[1])
    add_set(0)
    for sign in (-1, 1):
        take(source(sign, 0), 0)
        add_set(sign)
    spread_second(3)
    along(2)
    spread_second(half)
    add_set(-2)
    add_set(2)
    along(3)
    for sign in (-1, 1):
        take(source(3 * sign, 0), 0)
        add_set(3 * sign)
    work(8)
    for dx in range(NX):
        take(source(half, -dx), 0)
        work(1)
    add_set(half)
    work(len(ready))
    wait_bytes(dfull.at[pl.ds(0, NC - 1)], dsend)
    wait_bytes(nfull.at[pl.ds(0, NR - 1)], nsem.at[0])

    def send_all(src, dst, sems, group, size):
        for k in range(1, size):
            remote(src, dst.at[k - 1], sems.at[0], sems.at[1], group(k)).start()

    def lse(own, others, n):
        high = own
        for k in range(n):
            high = jnp.maximum(high, others[k])
        total = jnp.exp2(own - high)
        for k in range(n):
            total = total + jnp.exp2(others[k] - high)
        return high + log2(total)

    def add(own, others, n):
        for k in range(n):
            own = own + others[k]
        return own

    def rows_out(t, h):
        send_all(rsrc.at[t, h], rdst.at[t, h], rsem.at[t, h], row_peer, NR)

    def rows_in(t, h, combine):
        dst = rdst.at[t, h]
        wait_bytes(dst, rsem.at[t, h, 1])
        wait_bytes(dst, rsem.at[t, h, 0])
        return combine(rsrc[t, h], dst, NR - 1)

    def over_cols(t, combine):
        send_all(csrc.at[t, 1], cdstz.at[t, 0], csem.at[t, 1], z_peer, NZ)
        send_all(csrc.at[t, 0], cdstx.at[t, 0], csem.at[t, 0], x_peer, NX)
        wait_bytes(cdstx.at[t, 0], csem.at[t, 0, 1])
        cmid[t, 0] = combine(csrc[t, 0], cdstx.at[t, 0], NX - 1)
        send_all(cmid.at[t, 0], cdstz.at[t, 1], csem.at[t, 2], z_peer, NZ)
        wait_bytes(cdstz.at[t, 0], csem.at[t, 1, 1])
        cmid[t, 1] = combine(csrc[t, 1], cdstz.at[t, 0], NZ - 1)
        send_all(cmid.at[t, 1], cdstx.at[t, 1], csem.at[t, 3], x_peer, NX)
        wait_bytes(cdstz.at[t, 1], csem.at[t, 2, 1])
        first = combine(cmid[t, 0], cdstz.at[t, 1], NZ - 1)
        wait_bytes(cdstx.at[t, 1], csem.at[t, 3, 1])
        second = combine(cmid[t, 1], cdstx.at[t, 1], NX - 1)
        wait_bytes(cdstx.at[t, 0], csem.at[t, 0, 0])
        wait_bytes(cdstz.at[t, 0], csem.at[t, 1, 0])
        wait_bytes(cdstz.at[t, 1], csem.at[t, 2, 0])
        wait_bytes(cdstx.at[t, 1], csem.at[t, 3, 0])
        return first, second

    hr = NR // 2
    for h in range(2):
        for b in range(hr):
            rows = pl.ds((h * hr + b) * B, B)
            high = top[rows, :].T
            row_top = jnp.max(high, axis=0, keepdims=True)
            total = jnp.sum(acc[rows, :].T * jnp.exp2(high - row_top), axis=0, keepdims=True)
            rsrc[0, h, b:b + 1, :] = row_top + log2(total)
        rows_out(0, h)

    def widen(h, values):
        for b in range(hr):
            uwide[pl.ds((h * hr + b) * B, B), :] = spread(values[b:b + 1, :])


    fold = (SWEEP // 8, 8, B)
    steps = ROWS // SWEEP // 2
    zeros = (jnp.zeros((8, B), F32),) * NC

    def top_step(i, highs):
        rows = pl.ds(pl.multiple_of(i * SWEEP, SWEEP), SWEEP)
        u = uwide[rows, :]
        return tuple(
            jnp.maximum(high, jnp.max((tile[j, rows, :] + u).reshape(fold), axis=0)) for j, high in enumerate(highs)
        )

    highs = (jnp.full((8, B), -1e30, F32),) * NC
    for h in range(2):
        widen(h, -rows_in(0, h, lse))
        highs = lax.fori_loop(h * steps, (h + 1) * steps, top_step, highs)
    for j in range(NC):
        high = jnp.max(highs[j], axis=0, keepdims=True)
        colm[j:j + 1, :] = high
        high8[j] = jnp.broadcast_to(high - SHIFT, (8, B))

    def exp_step(i, totals):
        rows = pl.ds(pl.multiple_of(i * SWEEP, SWEEP), SWEEP)
        u = uwide[rows, :].reshape(fold)
        sums = []
        for j in range(NC):
            e = jnp.exp2(tile[j, rows, :].reshape(fold) + (u - high8[j]))
            tile[j, rows, :] = e.reshape(SWEEP, B)
            sums.append(totals[j] + jnp.sum(e, axis=0))
        return tuple(sums)

    totals = lax.fori_loop(0, ROWS // SWEEP, exp_step, zeros)
    for j in range(NC):
        colc[j:j + 1, :] = jnp.sum(totals[j], axis=0, keepdims=True)
    hc = NC // 2
    csrc[0] = (colm[...] + (log2(colc[...]) - SHIFT)).reshape(2, hc, B)
    for h, logs in enumerate(over_cols(0, lse)):
        half = pl.ds(h * hc, hc)
        colw[half, :] = jnp.exp2(colm[half, :] - logs + SHIFT)
        colv[half, :] = colw[half, :]

    def iteration(t, carry):
        def rows_pass(i, carry):
            rows = pl.ds(pl.multiple_of(i * 2 * B, 2 * B), 2 * B)
            total = tile[0, rows, :] * colv[0:1, :]
            for j in range(1, NC):
                total = total + tile[j, rows, :] * colv[j:j + 1, :]
            acc[rows, :] = total
            return carry

        for h in range(2):
            lax.fori_loop(h * hr // 2, (h + 1) * hr // 2, rows_pass, 0)
            for b in range(hr):
                rsrc[t, h, b:b + 1, :] = lanes_to_vector(acc[pl.ds((h * hr + b) * B, B), :])
            rows_out(t, h)

        def step(i, totals):
            rows = pl.ds(pl.multiple_of(i * SWEEP, SWEEP), SWEEP)
            u = uwide[rows, :]
            return tuple(
                total + jnp.sum((tile[j, rows, :] * u).reshape(fold), axis=0) for j, total in enumerate(totals)
            )

        totals = zeros
        for h in range(2):
            widen(h, 1.0 / rows_in(t, h, add))
            totals = lax.fori_loop(h * steps, (h + 1) * steps, step, totals)
        for j in range(NC):
            colc[j:j + 1, :] = jnp.sum(totals[j], axis=0, keepdims=True)
        csrc[t] = (colc[...] * colw[...]).reshape(2, hc, B)
        for h, sums in enumerate(over_cols(t, add)):
            half = pl.ds(h * hc, hc)
            colv[half, :] = colw[half, :] / sums
        return carry

    lax.fori_loop(1, ITERS, iteration, 0)

    y = r // 2
    core = lax.rem(r, 2)
    partner = (2 * y + 1 - core, c)

    def target(i):
        return lax.rem(y + 6 - i + 3 * (i // 2) + 2 * (i // 3), NR // 2)

    def weigh(i):
        q = target(i)
        rows = pl.ds(pl.multiple_of(q * 2 * B, 2 * B), 2 * B)
        n = total = None
        for g in range(0, NC, GROUP):
            parts = []
            for j in range(g, g + GROUP):
                w = (tile[j, rows, :] * colv[j:j + 1, :]).astype(BF16)
                parts.append(w)
                wide = w.astype(F32)
                total = wide if total is None else total + wide
            part = jnp.dot(
                jnp.concatenate(parts, axis=1),
                dfull[pl.ds(g, GROUP)].reshape(GROUP * B, D),
                preferred_element_type=F32,
            )
            n = part if n is None else n + part
        for h in range(2):
            num[i, h, 0:B] = n[h * B:(h + 1) * B]
            sums = lanes_to_vector(total[h * B:(h + 1) * B])
            num[i, h, B:B + 8, 0:B] = jnp.broadcast_to(sums, (8, B))
            num[i, h, B:B + 8, B:D] = jnp.zeros((8, B), F32)
        remote(num.at[i, 1 - core], pair.at[i], psem.at[0, i], psem.at[1, i], partner).start()

    def join(i):
        wait_bytes(pair.at[i], psem.at[1, i])
        num[i, core] = num[i, core] + pair[i]

    def hand_over(i):
        join(i)
        q = target(i)
        remote(num.at[i, core], numr.at[i], fsem.at[0], fsem.at[1], (2 * q + core, c)).start()

    weigh(0)

    def final(i, carry):
        weigh(i)
        hand_over(i - 1)
        return carry

    last = NR // 2 - 1
    lax.fori_loop(1, last + 1, final, 0)
    join(last)
    wait_bytes(numr, fsem.at[1])
    total = num[last, core]
    for k in range(last):
        total = total + numr[k]
    scale = spread(total[B:B + 1, 0:B])
    out[:, 0:B] = total[0:B, 0:B] / scale
    out[:, B:D] = total[0:B, B:D] / scale
    wait_bytes(numr, fsem.at[0])
    for i in range(last + 1):
        wait_bytes(pair.at[i], psem.at[0, i])


def solution(mesh):
    vmem, dma = pltpu.VMEM, pltpu.SemaphoreType.DMA
    scratch = [
        vmem((NC, ROWS, B), F32),
        vmem((NC, B, D), BF16),
        vmem((NR, B, D), BF16),
        vmem((ROWS, B), F32),
        vmem((ROWS, B), F32),
        vmem((ROWS, B), F32),
        vmem((NC, B), F32),
        vmem((NC, B), F32),
        vmem((NC, B), F32),
        vmem((NC, B), F32),
        vmem((NC, 8, B), F32),
        vmem((ITERS, 2, NR // 2, B), F32),
        vmem((ITERS, 2, NR - 1, NR // 2, B), F32),
        vmem((ITERS, 2, NC // 2, B), F32),
        vmem((ITERS, 2, NC // 2, B), F32),
        vmem((ITERS, 2, NX - 1, NC // 2, B), F32),
        vmem((ITERS, 2, NZ - 1, NC // 2, B), F32),
        vmem((NR // 2, 2, B + 8, D), F32),
        vmem((NR // 2, B + 8, D), F32),
        vmem((NR // 2 - 1, B + 8, D), F32),
        dma((2,)),
        dma((2,)),
        dma,
        dma((2, NC)),
        dma((ITERS, 2, 2)),
        dma((ITERS, 4, 2)),
        dma((2, NR // 2)),
        dma((2,)),
    ]

    def per_device(noise, data):
        return pl.pallas_call(
            kernel,
            out_shape=jax.ShapeDtypeStruct((B, D), F32),
            in_specs=[pl.BlockSpec(memory_space=pl.ANY)] * 2,
            out_specs=pl.BlockSpec(memory_space=pltpu.VMEM),
            scratch_shapes=scratch,
            compiler_params=pltpu.CompilerParams(
                collective_id=0, has_side_effects=True, vmem_limit_bytes=40 << 20
            ),
        )(noise, data)

    return jax.shard_map(
        per_device,
        mesh=mesh,
        in_specs=(P(("rows", "cols"), None), P(("cols", "rows"), None)),
        out_specs=P(("rows", "cols"), None),
        check_vma=False,
    )
```

```python
import functools
import math

import jax
import jax.numpy as jnp
from jax import lax
from jax.experimental import pallas as pl
from jax.experimental.pallas import tpu as pltpu
from jax.sharding import PartitionSpec as P

MESH = pl.DeviceIdType.MESH
F32 = jnp.float32
BF16 = jnp.bfloat16

ITERS = 4
NR = 8
NZ, NX = 8, 4
NC = NZ * NX
B = 128
D = 256
SPLIT = 48
ROWS = NR * B
CHUNK = 64
SWEEP = 32
GROUP = 8
SHIFT = 20.0
TO_LOG2 = 2.0 / math.log(2.0)
INV_LN2 = 1.0 / math.log(2.0)


def log2(v):
    return jnp.log(v) * INV_LN2


def wait_bytes(ref, sem):
    pltpu.make_async_copy(ref, ref, sem).wait()


def lanes_to_vector(block):
    return jnp.sum(block.T, axis=0, keepdims=True)


def spread(vec):
    return jnp.broadcast_to(vec, (B, B)).T


def kernel(
    noise, data, out,
    tile, dfull, nfull, top, acc, uwide, colw, colv, colc, colm, high8,
    rsrc, rdst, csrc, cmid, cdstx, cdstz, num, pair, numr,
    own_sem, nsem, dsend, drecv, rsem, csem, psem, fsem,
):
    r = lax.axis_index("rows")
    c = lax.axis_index("cols")
    z = c // NX
    x = lax.rem(c, NX)

    def row_peer(k):
        return (lax.rem(r + k, NR), c)

    def x_peer(k):
        return (r, z * NX + lax.rem(x + k, NX))

    def z_peer(k):
        return (r, lax.rem(z + k, NZ) * NX + x)

    own_d = pltpu.make_async_copy(data, dfull.at[c], own_sem.at[0])
    own_d.start()
    own_n = pltpu.make_async_copy(noise, nfull.at[r], own_sem.at[1])
    own_n.start()
    top[...] = jnp.full_like(top, -1e30)
    acc[...] = jnp.zeros_like(acc)

    barrier = pltpu.get_barrier_semaphore()
    peers = [row_peer(k) for k in range(1, NR)]
    peers += [x_peer(k) for k in range(1, NX)] + [z_peer(k) for k in range(1, NZ)]
    for peer in peers:
        pl.semaphore_signal(barrier, inc=1, device_id=peer, device_id_type=MESH)
    own_d.wait()
    own_n.wait()
    pl.semaphore_wait(barrier, len(peers))

    def remote(src, dst, send, recv, peer):
        return pltpu.make_async_remote_copy(
            src_ref=src, dst_ref=dst, send_sem=send, recv_sem=recv, device_id=peer, device_id_type=MESH
        )

    def part(block, h):
        return dfull.at[block, pl.ds(h * SPLIT, SPLIT + h * (B - 2 * SPLIT))]

    def give(block, h, peer):
        remote(part(block, h), part(block, h), dsend, drecv.at[h, block], peer).start()

    def take(block, h):
        wait_bytes(part(block, h), drecv.at[h, block])

    def source(dz, dx):
        return lax.rem(z + dz + NZ, NZ) * NX + lax.rem(x + dx + NX, NX)

    def across(block):
        for k in range(1, NX):
            give(block, 1, x_peer(k))

    for h in (0, 1):
        for k in range(1, NX):
            give(c, h, x_peer(k))
        for k in (2, NZ - 2, 1, NZ - 1):
            give(c, 1 - h, z_peer(k))
    for k in range(1, NR):
        remote(nfull.at[r], nfull.at[r], nsem.at[0], nsem.at[1], row_peer(k)).start()

    def scores(dz, i):
        base = pl.multiple_of(lax.rem(z + dz + NZ, NZ) * NX, NX)
        right = dfull[pl.ds(base, NX)].reshape(NX * B, D)
        left = nfull[pl.ds(2 * i, 2)].reshape(2 * B, D)
        s = lax.dot_general(left, right, (((1,), (1,)), ((), ())), preferred_element_type=F32)
        s = s * (D ** -0.5 * TO_LOG2)
        for k in range(0, 2 * B, CHUNK):
            rows = pl.ds(i * 2 * B + k, CHUNK)
            part = [s[k:k + CHUNK, j * B:(j + 1) * B] for j in range(NX)]
            for j in range(NX):
                tile[base + j, rows, :] = part[j]
            old = top[rows, :]
            new = jnp.maximum(old, jnp.maximum(jnp.maximum(part[0], part[1]), jnp.maximum(part[2], part[3])))
            total = acc[rows, :] * jnp.exp2(old - new)
            for j in range(NX):
                total = total + jnp.exp2(part[j] - new)
            top[rows, :] = new
            acc[rows, :] = total

    ready = []

    def work(count):
        for _ in range(min(count, len(ready))):
            ready.pop(0)()

    def add_set(dz):
        def rest():
            for dx in range(1, NX):
                take(source(dz, -dx), 1)
            scores(dz, 0)

        ready.append(rest)
        for i in range(1, NR // 2):
            ready.append(functools.partial(scores, dz, i))

    half = NZ // 2
    others = (1, 3, 2)

    def far(h, turn):
        for sign in (-1, 1):
            block = source(2 * sign, 0)
            take(block, h)
            if sign == turn:
                give(block, h, z_peer((NZ - 2 * sign) % NZ))
            give(block, h, z_peer((NZ - sign) % NZ))
            if h:
                across(block)

    def along(d):
        for dx in others:
            for sign in (-1, 1):
                block = source(d * sign, -dx)
                take(block, 0)
                if d < half - 1 or (dx != 2) == (sign < 0):
                    give(block, 0, z_peer((NZ - sign) % NZ))
                work(1)

    def spread_second(d):
        for sign in (-1, 1)[:2 if d < half else 1]:
            block = source(d * sign, 0)
            take(block, 1)
            across(block)
            work(1)

    for dx in others:
        block = source(0, -dx)
        take(block, 0)
        give(block, 0, z_peer(1))
        give(block, 0, z_peer(NZ - 1))
    spread_second(1)
    far(1, 1)
    far(0, -1)
    along(1)
    wait_bytes(nfull.at[pl.ds(0, NR - 1)], nsem.at[1])
    add_set(0)
    for sign in (-1, 1):
        take(source(sign, 0), 0)
        add_set(sign)
    spread_second(3)
    along(2)
    spread_second(half)
    add_set(-2)
    add_set(2)
    along(3)
    for sign in (-1, 1):
        take(source(3 * sign, 0), 0)
        add_set(3 * sign)
    work(8)
    for dx in range(NX):
        take(source(half, -dx), 0)
        work(1)
    add_set(half)
    work(len(ready))
    wait_bytes(dfull.at[pl.ds(0, NC - 1)], dsend)
    wait_bytes(nfull.at[pl.ds(0, NR - 1)], nsem.at[0])

    def send_all(src, dst, sems, group, size):
        for k in sorted(range(1, size), key=lambda k: abs(k - size // 2)):
            remote(src, dst.at[k - 1], sems.at[0], sems.at[1], group(k)).start()

    def lse(own, others, n):
        high = own
        for k in range(n):
            high = jnp.maximum(high, others[k])
        total = jnp.exp2(own - high)
        for k in range(n):
            total = total + jnp.exp2(others[k] - high)
        return high + log2(total)

    def add(own, others, n):
        for k in range(n):
            own = own + others[k]
        return own

    def rows_out(t, h):
        send_all(rsrc.at[t, h], rdst.at[t, h], rsem.at[t, h], row_peer, NR)

    def rows_in(t, h, combine):
        dst = rdst.at[t, h]
        wait_bytes(dst, rsem.at[t, h, 1])
        wait_bytes(dst, rsem.at[t, h, 0])
        return combine(rsrc[t, h], dst, NR - 1)

    def over_cols(t, combine):
        send_all(csrc.at[t, 1], cdstz.at[t, 0], csem.at[t, 1], z_peer, NZ)
        send_all(csrc.at[t, 0], cdstx.at[t, 0], csem.at[t, 0], x_peer, NX)
        wait_bytes(cdstx.at[t, 0], csem.at[t, 0, 1])
        cmid[t, 0] = combine(csrc[t, 0], cdstx.at[t, 0], NX - 1)
        send_all(cmid.at[t, 0], cdstz.at[t, 1], csem.at[t, 2], z_peer, NZ)
        wait_bytes(cdstz.at[t, 0], csem.at[t, 1, 1])
        cmid[t, 1] = combine(csrc[t, 1], cdstz.at[t, 0], NZ - 1)
        send_all(cmid.at[t, 1], cdstx.at[t, 1], csem.at[t, 3], x_peer, NX)
        wait_bytes(cdstz.at[t, 1], csem.at[t, 2, 1])
        first = combine(cmid[t, 0], cdstz.at[t, 1], NZ - 1)
        wait_bytes(cdstx.at[t, 1], csem.at[t, 3, 1])
        second = combine(cmid[t, 1], cdstx.at[t, 1], NX - 1)
        wait_bytes(cdstx.at[t, 0], csem.at[t, 0, 0])
        wait_bytes(cdstz.at[t, 0], csem.at[t, 1, 0])
        wait_bytes(cdstz.at[t, 1], csem.at[t, 2, 0])
        wait_bytes(cdstx.at[t, 1], csem.at[t, 3, 0])
        return first, second

    hr = NR // 2
    for h in range(2):
        for b in range(hr):
            rows = pl.ds((h * hr + b) * B, B)
            high = top[rows, :].T
            row_top = jnp.max(high, axis=0, keepdims=True)
            total = jnp.sum(acc[rows, :].T * jnp.exp2(high - row_top), axis=0, keepdims=True)
            rsrc[0, h, b:b + 1, :] = row_top + log2(total)
        rows_out(0, h)

    def widen(h, values):
        for b in range(hr):
            uwide[pl.ds((h * hr + b) * B, B), :] = spread(values[b:b + 1, :])


    fold = (SWEEP // 8, 8, B)
    steps = ROWS // SWEEP // 2
    zeros = (jnp.zeros((8, B), F32),) * NC

    def top_step(i, highs):
        rows = pl.ds(pl.multiple_of(i * SWEEP, SWEEP), SWEEP)
        u = uwide[rows, :]
        return tuple(
            jnp.maximum(high, jnp.max((tile[j, rows, :] + u).reshape(fold), axis=0)) for j, high in enumerate(highs)
        )

    highs = (jnp.full((8, B), -1e30, F32),) * NC
    for h in range(2):
        widen(h, -rows_in(0, h, lse))
        highs = lax.fori_loop(h * steps, (h + 1) * steps, top_step, highs)
    for j in range(NC):
        high = jnp.max(highs[j], axis=0, keepdims=True)
        colm[j:j + 1, :] = high
        high8[j] = jnp.broadcast_to(high - SHIFT, (8, B))

    def exp_step(i, totals):
        rows = pl.ds(pl.multiple_of(i * SWEEP, SWEEP), SWEEP)
        u = uwide[rows, :].reshape(fold)
        sums = []
        for j in range(NC):
            e = jnp.exp2(tile[j, rows, :].reshape(fold) + (u - high8[j]))
            tile[j, rows, :] = e.reshape(SWEEP, B)
            sums.append(totals[j] + jnp.sum(e, axis=0))
        return tuple(sums)

    totals = lax.fori_loop(0, ROWS // SWEEP, exp_step, zeros)
    for j in range(NC):
        colc[j:j + 1, :] = jnp.sum(totals[j], axis=0, keepdims=True)
    hc = NC // 2
    csrc[0] = (colm[...] + (log2(colc[...]) - SHIFT)).reshape(2, hc, B)
    for h, logs in enumerate(over_cols(0, lse)):
        half = pl.ds(h * hc, hc)
        colw[half, :] = jnp.exp2(colm[half, :] - logs + SHIFT)
        colv[half, :] = colw[half, :]

    def iteration(t, carry):
        def rows_pass(i, carry):
            rows = pl.ds(pl.multiple_of(i * 2 * B, 2 * B), 2 * B)
            total = tile[0, rows, :] * colv[0:1, :]
            for j in range(1, NC):
                total = total + tile[j, rows, :] * colv[j:j + 1, :]
            acc[rows, :] = total
            return carry

        for h in range(2):
            lax.fori_loop(h * hr // 2, (h + 1) * hr // 2, rows_pass, 0)
            for b in range(hr):
                rsrc[t, h, b:b + 1, :] = lanes_to_vector(acc[pl.ds((h * hr + b) * B, B), :])
            rows_out(t, h)

        def step(i, totals):
            rows = pl.ds(pl.multiple_of(i * SWEEP, SWEEP), SWEEP)
            u = uwide[rows, :]
            return tuple(
                total + jnp.sum((tile[j, rows, :] * u).reshape(fold), axis=0) for j, total in enumerate(totals)
            )

        totals = zeros
        for h in range(2):
            widen(h, 1.0 / rows_in(t, h, add))
            totals = lax.fori_loop(h * steps, (h + 1) * steps, step, totals)
        for j in range(NC):
            colc[j:j + 1, :] = jnp.sum(totals[j], axis=0, keepdims=True)
        csrc[t] = (colc[...] * colw[...]).reshape(2, hc, B)
        for h, sums in enumerate(over_cols(t, add)):
            half = pl.ds(h * hc, hc)
            colv[half, :] = colw[half, :] / sums
        return carry

    lax.fori_loop(1, ITERS, iteration, 0)

    y = r // 2
    core = lax.rem(r, 2)
    partner = (2 * y + 1 - core, c)

    def target(i):
        return lax.rem(y + 6 - i + 3 * (i // 2) + 2 * (i // 3), NR // 2)

    def weigh(i):
        q = target(i)
        rows = pl.ds(pl.multiple_of(q * 2 * B, 2 * B), 2 * B)
        n = total = None
        for g in range(0, NC, GROUP):
            parts = []
            for j in range(g, g + GROUP):
                w = (tile[j, rows, :] * colv[j:j + 1, :]).astype(BF16)
                parts.append(w)
                wide = w.astype(F32)
                total = wide if total is None else total + wide
            part = jnp.dot(
                jnp.concatenate(parts, axis=1),
                dfull[pl.ds(g, GROUP)].reshape(GROUP * B, D),
                preferred_element_type=F32,
            )
            n = part if n is None else n + part
        for h in range(2):
            num[i, h, 0:B] = n[h * B:(h + 1) * B]
            sums = lanes_to_vector(total[h * B:(h + 1) * B])
            num[i, h, B:B + 8, 0:B] = jnp.broadcast_to(sums, (8, B))
            num[i, h, B:B + 8, B:D] = jnp.zeros((8, B), F32)
        remote(num.at[i, 1 - core], pair.at[i], psem.at[0, i], psem.at[1, i], partner).start()

    def join(i):
        wait_bytes(pair.at[i], psem.at[1, i])
        num[i, core] = num[i, core] + pair[i]

    def hand_over(i):
        join(i)
        q = target(i)
        remote(num.at[i, core], numr.at[i], fsem.at[0], fsem.at[1], (2 * q + core, c)).start()

    weigh(0)

    def final(i, carry):
        weigh(i)
        hand_over(i - 1)
        return carry

    last = NR // 2 - 1
    lax.fori_loop(1, last + 1, final, 0)
    join(last)
    wait_bytes(numr, fsem.at[1])
    total = num[last, core]
    for k in range(last):
        total = total + numr[k]
    scale = spread(total[B:B + 1, 0:B])
    out[:, 0:B] = total[0:B, 0:B] / scale
    out[:, B:D] = total[0:B, B:D] / scale
    wait_bytes(numr, fsem.at[0])
    for i in range(last + 1):
        wait_bytes(pair.at[i], psem.at[0, i])


def solution(mesh):
    vmem, dma = pltpu.VMEM, pltpu.SemaphoreType.DMA
    scratch = [
        vmem((NC, ROWS, B), F32),
        vmem((NC, B, D), BF16),
        vmem((NR, B, D), BF16),
        vmem((ROWS, B), F32),
        vmem((ROWS, B), F32),
        vmem((ROWS, B), F32),
        vmem((NC, B), F32),
        vmem((NC, B), F32),
        vmem((NC, B), F32),
        vmem((NC, B), F32),
        vmem((NC, 8, B), F32),
        vmem((ITERS, 2, NR // 2, B), F32),
        vmem((ITERS, 2, NR - 1, NR // 2, B), F32),
        vmem((ITERS, 2, NC // 2, B), F32),
        vmem((ITERS, 2, NC // 2, B), F32),
        vmem((ITERS, 2, NX - 1, NC // 2, B), F32),
        vmem((ITERS, 2, NZ - 1, NC // 2, B), F32),
        vmem((NR // 2, 2, B + 8, D), F32),
        vmem((NR // 2, B + 8, D), F32),
        vmem((NR // 2 - 1, B + 8, D), F32),
        dma((2,)),
        dma((2,)),
        dma,
        dma((2, NC)),
        dma((ITERS, 2, 2)),
        dma((ITERS, 4, 2)),
        dma((2, NR // 2)),
        dma((2,)),
    ]

    def per_device(noise, data):
        return pl.pallas_call(
            kernel,
            out_shape=jax.ShapeDtypeStruct((B, D), F32),
            in_specs=[pl.BlockSpec(memory_space=pl.ANY)] * 2,
            out_specs=pl.BlockSpec(memory_space=pltpu.VMEM),
            scratch_shapes=scratch,
            compiler_params=pltpu.CompilerParams(
                collective_id=0, has_side_effects=True, vmem_limit_bytes=40 << 20
            ),
        )(noise, data)

    return jax.shard_map(
        per_device,
        mesh=mesh,
        in_specs=(P(("rows", "cols"), None), P(("cols", "rows"), None)),
        out_specs=P(("rows", "cols"), None),
        check_vma=False,
    )
```

```python
import functools
import math

import jax
import jax.numpy as jnp
from jax import lax
from jax.experimental import pallas as pl
from jax.experimental.pallas import tpu as pltpu
from jax.sharding import PartitionSpec as P

MESH = pl.DeviceIdType.MESH
F32 = jnp.float32
BF16 = jnp.bfloat16

ITERS = 4
NR = 8
NZ, NX = 8, 4
NC = NZ * NX
B = 128
D = 256
SPLIT = 48
ROWS = NR * B
CHUNK = 64
SWEEP = 32
GROUP = 8
SHIFT = 20.0
TO_LOG2 = 2.0 / math.log(2.0)
INV_LN2 = 1.0 / math.log(2.0)


def log2(v):
    return jnp.log(v) * INV_LN2


def wait_bytes(ref, sem):
    pltpu.make_async_copy(ref, ref, sem).wait()


def lanes_to_vector(block):
    return jnp.sum(block.T, axis=0, keepdims=True)


def spread(vec):
    return jnp.broadcast_to(vec, (B, B)).T


def kernel(
    noise, data, out,
    tile, dfull, nfull, top, acc, uwide, colw, colv, colc, colm, high8,
    rsrc, rdst, csrc, cmid, cdstx, cdstz, num, pair, numr,
    own_sem, nsem, dsend, drecv, rsem, csem, psem, fsem,
):
    r = lax.axis_index("rows")
    c = lax.axis_index("cols")
    z = c // NX
    x = lax.rem(c, NX)

    def row_peer(k):
        return (lax.rem(r + k, NR), c)

    def x_peer(k):
        return (r, z * NX + lax.rem(x + k, NX))

    def z_peer(k):
        return (r, lax.rem(z + k, NZ) * NX + x)

    own_d = pltpu.make_async_copy(data, dfull.at[c], own_sem.at[0])
    own_d.start()
    own_n = pltpu.make_async_copy(noise, nfull.at[r], own_sem.at[1])
    own_n.start()
    top[...] = jnp.full_like(top, -1e30)
    acc[...] = jnp.zeros_like(acc)

    barrier = pltpu.get_barrier_semaphore()
    peers = [row_peer(k) for k in range(1, NR)]
    peers += [x_peer(k) for k in range(1, NX)] + [z_peer(k) for k in range(1, NZ)]
    for peer in peers:
        pl.semaphore_signal(barrier, inc=1, device_id=peer, device_id_type=MESH)
    own_d.wait()
    own_n.wait()
    pl.semaphore_wait(barrier, len(peers))

    def remote(src, dst, send, recv, peer):
        return pltpu.make_async_remote_copy(
            src_ref=src, dst_ref=dst, send_sem=send, recv_sem=recv, device_id=peer, device_id_type=MESH
        )

    def part(block, h):
        return dfull.at[block, pl.ds(h * SPLIT, SPLIT + h * (B - 2 * SPLIT))]

    def give(block, h, peer):
        remote(part(block, h), part(block, h), dsend, drecv.at[h, block], peer).start()

    def take(block, h):
        wait_bytes(part(block, h), drecv.at[h, block])

    def source(dz, dx):
        return lax.rem(z + dz + NZ, NZ) * NX + lax.rem(x + dx + NX, NX)

    def across(block):
        for k in range(1, NX):
            give(block, 1, x_peer(k))

    for h in (0, 1):
        for k in range(1, NX):
            give(c, h, x_peer(k))
        for k in (2, NZ - 2, 1, NZ - 1):
            give(c, 1 - h, z_peer(k))
    for k in range(1, NR):
        remote(nfull.at[r], nfull.at[r], nsem.at[0], nsem.at[1], row_peer(k)).start()

    def scores(dz, i):
        base = pl.multiple_of(lax.rem(z + dz + NZ, NZ) * NX, NX)
        right = dfull[pl.ds(base, NX)].reshape(NX * B, D)
        left = nfull[pl.ds(2 * i, 2)].reshape(2 * B, D)
        s = lax.dot_general(left, right, (((1,), (1,)), ((), ())), preferred_element_type=F32)
        s = s * (D ** -0.5 * TO_LOG2)
        for k in range(0, 2 * B, CHUNK):
            rows = pl.ds(i * 2 * B + k, CHUNK)
            part = [s[k:k + CHUNK, j * B:(j + 1) * B] for j in range(NX)]
            for j in range(NX):
                tile[base + j, rows, :] = part[j]
            old = top[rows, :]
            new = jnp.maximum(old, jnp.maximum(jnp.maximum(part[0], part[1]), jnp.maximum(part[2], part[3])))
            total = acc[rows, :] * jnp.exp2(old - new)
            for j in range(NX):
                total = total + jnp.exp2(part[j] - new)
            top[rows, :] = new
            acc[rows, :] = total

    ready = []

    def work(count):
        for _ in range(min(count, len(ready))):
            ready.pop(0)()

    def add_set(dz):
        def rest():
            for dx in range(1, NX):
                take(source(dz, -dx), 1)
            scores(dz, 0)

        ready.append(rest)
        for i in range(1, NR // 2):
            ready.append(functools.partial(scores, dz, i))

    half = NZ // 2
    others = (1, 3, 2)

    def far(h, turn):
        for sign in (-1, 1):
            block = source(2 * sign, 0)
            take(block, h)
            if sign == turn:
                give(block, h, z_peer((NZ - 2 * sign) % NZ))
            give(block, h, z_peer((NZ - sign) % NZ))
            if h:
                across(block)

    def along(d):
        for dx in others:
            for sign in (-1, 1):
                block = source(d * sign, -dx)
                take(block, 0)
                if d < half - 1 or (dx != 2) == (sign < 0):
                    give(block, 0, z_peer((NZ - sign) % NZ))
                work(1)

    def spread_second(d):
        for sign in (-1, 1)[:2 if d < half else 1]:
            block = source(d * sign, 0)
            take(block, 1)
            across(block)
            work(1)

    for dx in others:
        block = source(0, -dx)
        take(block, 0)
        give(block, 0, z_peer(1))
        give(block, 0, z_peer(NZ - 1))
    spread_second(1)
    far(1, 1)
    far(0, -1)
    along(1)
    wait_bytes(nfull.at[pl.ds(0, NR - 1)], nsem.at[1])
    add_set(0)
    for sign in (-1, 1):
        take(source(sign, 0), 0)
        add_set(sign)
    spread_second(3)
    along(2)
    spread_second(half)
    add_set(-2)
    add_set(2)
    along(3)
    for sign in (-1, 1):
        take(source(3 * sign, 0), 0)
        add_set(3 * sign)
    work(8)
    for dx in range(NX):
        take(source(half, -dx), 0)
        work(1)
    add_set(half)
    work(len(ready))
    wait_bytes(dfull.at[pl.ds(0, NC - 1)], dsend)
    wait_bytes(nfull.at[pl.ds(0, NR - 1)], nsem.at[0])

    def send_all(src, dst, sems, group, size):
        for k in sorted(range(1, size), key=lambda k: abs(k - size // 2)):
            remote(src, dst.at[k - 1], sems.at[0], sems.at[1], group(k)).start()

    def lse(own, others, n):
        high = own
        for k in range(n):
            high = jnp.maximum(high, others[k])
        total = jnp.exp2(own - high)
        for k in range(n):
            total = total + jnp.exp2(others[k] - high)
        return high + log2(total)

    def add(own, others, n):
        for k in range(n):
            own = own + others[k]
        return own

    def rows_out(t, h):
        send_all(rsrc.at[t, h], rdst.at[t, h], rsem.at[t, h], row_peer, NR)

    def rows_in(t, h, combine):
        dst = rdst.at[t, h]
        wait_bytes(dst, rsem.at[t, h, 1])
        wait_bytes(dst, rsem.at[t, h, 0])
        return combine(rsrc[t, h], dst, NR - 1)

    def over_cols(t, combine):
        send_all(csrc.at[t, 1], cdstz.at[t, 0], csem.at[t, 1], z_peer, NZ)
        send_all(csrc.at[t, 0], cdstx.at[t, 0], csem.at[t, 0], x_peer, NX)
        wait_bytes(cdstx.at[t, 0], csem.at[t, 0, 1])
        cmid[t, 0] = combine(csrc[t, 0], cdstx.at[t, 0], NX - 1)
        send_all(cmid.at[t, 0], cdstz.at[t, 1], csem.at[t, 2], z_peer, NZ)
        wait_bytes(cdstz.at[t, 0], csem.at[t, 1, 1])
        cmid[t, 1] = combine(csrc[t, 1], cdstz.at[t, 0], NZ - 1)
        send_all(cmid.at[t, 1], cdstx.at[t, 1], csem.at[t, 3], x_peer, NX)
        wait_bytes(cdstz.at[t, 1], csem.at[t, 2, 1])
        first = combine(cmid[t, 0], cdstz.at[t, 1], NZ - 1)
        wait_bytes(cdstx.at[t, 1], csem.at[t, 3, 1])
        second = combine(cmid[t, 1], cdstx.at[t, 1], NX - 1)
        wait_bytes(cdstx.at[t, 0], csem.at[t, 0, 0])
        wait_bytes(cdstz.at[t, 0], csem.at[t, 1, 0])
        wait_bytes(cdstz.at[t, 1], csem.at[t, 2, 0])
        wait_bytes(cdstx.at[t, 1], csem.at[t, 3, 0])
        return first, second

    hr = NR // 2
    for h in range(2):
        for b in range(hr):
            rows = pl.ds((h * hr + b) * B, B)
            high = top[rows, :].T
            row_top = jnp.max(high, axis=0, keepdims=True)
            total = jnp.sum(acc[rows, :].T * jnp.exp2(high - row_top), axis=0, keepdims=True)
            rsrc[0, h, b:b + 1, :] = row_top + log2(total)
        rows_out(0, h)

    def widen(h, values):
        for b in range(hr):
            uwide[pl.ds((h * hr + b) * B, B), :] = spread(values[b:b + 1, :])


    fold = (SWEEP // 8, 8, B)
    steps = ROWS // SWEEP // 2
    zeros = (jnp.zeros((8, B), F32),) * NC

    def top_step(i, highs):
        rows = pl.ds(pl.multiple_of(i * SWEEP, SWEEP), SWEEP)
        u = uwide[rows, :]
        return tuple(
            jnp.maximum(high, jnp.max((tile[j, rows, :] + u).reshape(fold), axis=0)) for j, high in enumerate(highs)
        )

    highs = (jnp.full((8, B), -1e30, F32),) * NC
    for h in range(2):
        widen(h, -rows_in(0, h, lse))
        highs = lax.fori_loop(h * steps, (h + 1) * steps, top_step, highs)
    for j in range(NC):
        high = jnp.max(highs[j], axis=0, keepdims=True)
        colm[j:j + 1, :] = high
        high8[j] = jnp.broadcast_to(high - SHIFT, (8, B))

    def exp_step(i, totals):
        rows = pl.ds(pl.multiple_of(i * SWEEP, SWEEP), SWEEP)
        u = uwide[rows, :].reshape(fold)
        sums = []
        for j in range(NC):
            e = jnp.exp2(tile[j, rows, :].reshape(fold) + (u - high8[j]))
            tile[j, rows, :] = e.reshape(SWEEP, B)
            sums.append(totals[j] + jnp.sum(e, axis=0))
        return tuple(sums)

    totals = lax.fori_loop(0, ROWS // SWEEP, exp_step, zeros)
    for j in range(NC):
        colc[j:j + 1, :] = jnp.sum(totals[j], axis=0, keepdims=True)
    hc = NC // 2
    csrc[0] = (colm[...] + (log2(colc[...]) - SHIFT)).reshape(2, hc, B)
    for h, logs in enumerate(over_cols(0, lse)):
        half = pl.ds(h * hc, hc)
        colw[half, :] = jnp.exp2(colm[half, :] - logs + SHIFT)
        colv[half, :] = colw[half, :]

    def iteration(t, carry):
        def rows_pass(i, carry):
            rows = pl.ds(pl.multiple_of(i * 2 * B, 2 * B), 2 * B)
            total = tile[0, rows, :] * colv[0:1, :]
            for j in range(1, NC):
                total = total + tile[j, rows, :] * colv[j:j + 1, :]
            acc[rows, :] = total
            return carry

        for h in range(2):
            lax.fori_loop(h * hr // 2, (h + 1) * hr // 2, rows_pass, 0)
            for b in range(hr):
                rsrc[t, h, b:b + 1, :] = lanes_to_vector(acc[pl.ds((h * hr + b) * B, B), :])
            rows_out(t, h)

        def step(i, totals):
            rows = pl.ds(pl.multiple_of(i * SWEEP, SWEEP), SWEEP)
            u = uwide[rows, :]
            return tuple(
                total + jnp.sum((tile[j, rows, :] * u).reshape(fold), axis=0) for j, total in enumerate(totals)
            )

        totals = zeros
        for h in range(2):
            widen(h, 1.0 / rows_in(t, h, add))
            totals = lax.fori_loop(h * steps, (h + 1) * steps, step, totals)
        for j in range(NC):
            colc[j:j + 1, :] = jnp.sum(totals[j], axis=0, keepdims=True)
        csrc[t] = (colc[...] * colw[...]).reshape(2, hc, B)
        for h, sums in enumerate(over_cols(t, add)):
            half = pl.ds(h * hc, hc)
            colv[half, :] = colw[half, :] / sums
        return carry

    lax.fori_loop(1, ITERS, iteration, 0)

    y = r // 2
    core = lax.rem(r, 2)
    partner = (2 * y + 1 - core, c)

    def target(i):
        return lax.rem(y + 6 - i + 3 * (i // 2) + 2 * (i // 3), NR // 2)

    def weigh(i):
        q = target(i)
        rows = pl.ds(pl.multiple_of(q * 2 * B, 2 * B), 2 * B)
        n = total = None
        for g in range(0, NC, GROUP):
            parts = []
            for j in range(g, g + GROUP):
                w = (tile[j, rows, :] * colv[j:j + 1, :]).astype(BF16)
                parts.append(w)
                wide = w.astype(F32)
                total = wide if total is None else total + wide
            part = jnp.dot(
                jnp.concatenate(parts, axis=1),
                dfull[pl.ds(g, GROUP)].reshape(GROUP * B, D),
                preferred_element_type=F32,
            )
            n = part if n is None else n + part
        for h in range(2):
            num[i, h, 0:B] = n[h * B:(h + 1) * B]
            sums = lanes_to_vector(total[h * B:(h + 1) * B])
            num[i, h, B:B + 8, 0:B] = jnp.broadcast_to(sums, (8, B))
            num[i, h, B:B + 8, B:D] = jnp.zeros((8, B), F32)
        remote(num.at[i, 1 - core], pair.at[i], psem.at[0, i], psem.at[1, i], partner).start()

    def join(i):
        wait_bytes(pair.at[i], psem.at[1, i])
        num[i, core] = num[i, core] + pair[i]

    def hand_over(i):
        join(i)
        q = target(i)
        remote(num.at[i, core], numr.at[i], fsem.at[0], fsem.at[1], (2 * q + core, c)).start()

    def first(i, carry):
        weigh(i)
        return carry

    last = NR // 2 - 1
    lax.fori_loop(0, last, first, 0)
    hand_over(0)
    hand_over(1)
    weigh(last)
    hand_over(2)
    join(last)
    wait_bytes(numr, fsem.at[1])
    total = num[last, core]
    for k in range(last):
        total = total + numr[k]
    scale = spread(total[B:B + 1, 0:B])
    out[:, 0:B] = total[0:B, 0:B] / scale
    out[:, B:D] = total[0:B, B:D] / scale
    wait_bytes(numr, fsem.at[0])
    for i in range(last + 1):
        wait_bytes(pair.at[i], psem.at[0, i])


def solution(mesh):
    vmem, dma = pltpu.VMEM, pltpu.SemaphoreType.DMA
    scratch = [
        vmem((NC, ROWS, B), F32),
        vmem((NC, B, D), BF16),
        vmem((NR, B, D), BF16),
        vmem((ROWS, B), F32),
        vmem((ROWS, B), F32),
        vmem((ROWS, B), F32),
        vmem((NC, B), F32),
        vmem((NC, B), F32),
        vmem((NC, B), F32),
        vmem((NC, B), F32),
        vmem((NC, 8, B), F32),
        vmem((ITERS, 2, NR // 2, B), F32),
        vmem((ITERS, 2, NR - 1, NR // 2, B), F32),
        vmem((ITERS, 2, NC // 2, B), F32),
        vmem((ITERS, 2, NC // 2, B), F32),
        vmem((ITERS, 2, NX - 1, NC // 2, B), F32),
        vmem((ITERS, 2, NZ - 1, NC // 2, B), F32),
        vmem((NR // 2, 2, B + 8, D), F32),
        vmem((NR // 2, B + 8, D), F32),
        vmem((NR // 2 - 1, B + 8, D), F32),
        dma((2,)),
        dma((2,)),
        dma,
        dma((2, NC)),
        dma((ITERS, 2, 2)),
        dma((ITERS, 4, 2)),
        dma((2, NR // 2)),
        dma((2,)),
    ]

    def per_device(noise, data):
        return pl.pallas_call(
            kernel,
            out_shape=jax.ShapeDtypeStruct((B, D), F32),
            in_specs=[pl.BlockSpec(memory_space=pl.ANY)] * 2,
            out_specs=pl.BlockSpec(memory_space=pltpu.VMEM),
            scratch_shapes=scratch,
            compiler_params=pltpu.CompilerParams(
                collective_id=0, has_side_effects=True, vmem_limit_bytes=40 << 20
            ),
        )(noise, data)

    return jax.shard_map(
        per_device,
        mesh=mesh,
        in_specs=(P(("rows", "cols"), None), P(("cols", "rows"), None)),
        out_specs=P(("rows", "cols"), None),
        check_vma=False,
    )
```

```python
import functools
import math

import jax
import jax.numpy as jnp
from jax import lax
from jax.experimental import pallas as pl
from jax.experimental.pallas import tpu as pltpu
from jax.sharding import PartitionSpec as P

MESH = pl.DeviceIdType.MESH
F32 = jnp.float32
BF16 = jnp.bfloat16

ITERS = 4
NR = 8
NZ, NX = 8, 4
NC = NZ * NX
B = 128
D = 256
SPLIT = 48
ROWS = NR * B
CHUNK = 64
SWEEP = 32
GROUP = 8
SHIFT = 20.0
TO_LOG2 = 2.0 / math.log(2.0)
INV_LN2 = 1.0 / math.log(2.0)


def log2(v):
    return jnp.log(v) * INV_LN2


def wait_bytes(ref, sem):
    pltpu.make_async_copy(ref, ref, sem).wait()


def lanes_to_vector(block):
    return jnp.sum(block.T, axis=0, keepdims=True)


def spread(vec):
    return jnp.broadcast_to(vec, (B, B)).T


def kernel(
    noise, data, out,
    tile, dfull, nfull, top, acc, uwide, colw, colv, colc, colm, high8,
    rsrc, rdst, csrc, cmid, cdstx, cdstz, num, pair, numr,
    own_sem, nsem, dsend, drecv, rsem, csem, psem, fsem,
):
    r = lax.axis_index("rows")
    c = lax.axis_index("cols")
    z = c // NX
    x = lax.rem(c, NX)

    def row_peer(k):
        return (lax.rem(r + k, NR), c)

    def x_peer(k):
        return (r, z * NX + lax.rem(x + k, NX))

    def z_peer(k):
        return (r, lax.rem(z + k, NZ) * NX + x)

    own_d = pltpu.make_async_copy(data, dfull.at[c], own_sem.at[0])
    own_d.start()
    own_n = pltpu.make_async_copy(noise, nfull.at[r], own_sem.at[1])
    own_n.start()
    top[...] = jnp.full_like(top, -1e30)
    acc[...] = jnp.zeros_like(acc)

    barrier = pltpu.get_barrier_semaphore()
    peers = [row_peer(k) for k in range(1, NR)]
    peers += [x_peer(k) for k in range(1, NX)] + [z_peer(k) for k in range(1, NZ)]
    for peer in peers:
        pl.semaphore_signal(barrier, inc=1, device_id=peer, device_id_type=MESH)
    own_d.wait()
    own_n.wait()
    pl.semaphore_wait(barrier, len(peers))

    def remote(src, dst, send, recv, peer):
        return pltpu.make_async_remote_copy(
            src_ref=src, dst_ref=dst, send_sem=send, recv_sem=recv, device_id=peer, device_id_type=MESH
        )

    def part(block, h):
        return dfull.at[block, pl.ds(h * SPLIT, SPLIT + h * (B - 2 * SPLIT))]

    def give(block, h, peer):
        remote(part(block, h), part(block, h), dsend, drecv.at[h, block], peer).start()

    def take(block, h):
        wait_bytes(part(block, h), drecv.at[h, block])

    def source(dz, dx):
        return lax.rem(z + dz + NZ, NZ) * NX + lax.rem(x + dx + NX, NX)

    def across(block):
        for k in range(1, NX):
            give(block, 1, x_peer(k))

    for h in (0, 1):
        for k in range(1, NX):
            give(c, h, x_peer(k))
        for k in (2, NZ - 2, 1, NZ - 1):
            give(c, 1 - h, z_peer(k))
    for k in range(1, NR):
        remote(nfull.at[r], nfull.at[r], nsem.at[0], nsem.at[1], row_peer(k)).start()

    def scores(dz, i):
        base = pl.multiple_of(lax.rem(z + dz + NZ, NZ) * NX, NX)
        right = dfull[pl.ds(base, NX)].reshape(NX * B, D)
        left = nfull[pl.ds(2 * i, 2)].reshape(2 * B, D)
        s = lax.dot_general(left, right, (((1,), (1,)), ((), ())), preferred_element_type=F32)
        s = s * (D ** -0.5 * TO_LOG2)
        for k in range(0, 2 * B, CHUNK):
            rows = pl.ds(i * 2 * B + k, CHUNK)
            part = [s[k:k + CHUNK, j * B:(j + 1) * B] for j in range(NX)]
            for j in range(NX):
                tile[base + j, rows, :] = part[j]
            old = top[rows, :]
            new = jnp.maximum(old, jnp.maximum(jnp.maximum(part[0], part[1]), jnp.maximum(part[2], part[3])))
            total = acc[rows, :] * jnp.exp2(old - new)
            for j in range(NX):
                total = total + jnp.exp2(part[j] - new)
            top[rows, :] = new
            acc[rows, :] = total

    ready = []

    def work(count):
        for _ in range(min(count, len(ready))):
            ready.pop(0)()

    def add_set(dz):
        def rest():
            for dx in range(1, NX):
                take(source(dz, -dx), 1)
            scores(dz, 0)

        ready.append(rest)
        for i in range(1, NR // 2):
            ready.append(functools.partial(scores, dz, i))

    half = NZ // 2
    others = (1, 3, 2)

    def far(h, turn):
        for sign in (-1, 1):
            block = source(2 * sign, 0)
            take(block, h)
            if sign == turn:
                give(block, h, z_peer((NZ - 2 * sign) % NZ))
            give(block, h, z_peer((NZ - sign) % NZ))
            if h:
                across(block)

    def along(d):
        for dx in others:
            for sign in (-1, 1):
                block = source(d * sign, -dx)
                take(block, 0)
                if d < half - 1 or (dx != 2) == (sign < 0):
                    give(block, 0, z_peer((NZ - sign) % NZ))
                work(1)

    def spread_second(d):
        for sign in (-1, 1)[:2 if d < half else 1]:
            block = source(d * sign, 0)
            take(block, 1)
            across(block)
            work(1)

    for dx in others:
        block = source(0, -dx)
        take(block, 0)
        give(block, 0, z_peer(1))
        give(block, 0, z_peer(NZ - 1))
    spread_second(1)
    far(1, 1)
    far(0, -1)
    along(1)
    wait_bytes(nfull.at[pl.ds(0, NR - 1)], nsem.at[1])
    add_set(0)
    for sign in (-1, 1):
        take(source(sign, 0), 0)
        add_set(sign)
    spread_second(3)
    along(2)
    spread_second(half)
    add_set(-2)
    add_set(2)
    along(3)
    for sign in (-1, 1):
        take(source(3 * sign, 0), 0)
        add_set(3 * sign)
    work(8)
    for dx in range(NX):
        take(source(half, -dx), 0)
        work(1)
    add_set(half)
    work(len(ready))

    def send_all(src, dst, sems, group, size):
        for k in sorted(range(1, size), key=lambda k: abs(k - size // 2)):
            remote(src, dst.at[k - 1], sems.at[0], sems.at[1], group(k)).start()

    def lse(own, others, n):
        high = own
        for k in range(n):
            high = jnp.maximum(high, others[k])
        total = jnp.exp2(own - high)
        for k in range(n):
            total = total + jnp.exp2(others[k] - high)
        return high + log2(total)

    def add(own, others, n):
        for k in range(n):
            own = own + others[k]
        return own

    def rows_out(t, h):
        send_all(rsrc.at[t, h], rdst.at[t, h], rsem.at[t, h], row_peer, NR)

    def rows_in(t, h, combine):
        dst = rdst.at[t, h]
        wait_bytes(dst, rsem.at[t, h, 1])
        return combine(rsrc[t, h], dst, NR - 1)

    def over_cols(t, combine):
        send_all(csrc.at[t, 0], cdstx.at[t, 0], csem.at[t, 0], x_peer, NX)
        send_all(csrc.at[t, 1], cdstz.at[t, 0], csem.at[t, 1], z_peer, NZ)
        wait_bytes(cdstx.at[t, 0], csem.at[t, 0, 1])
        cmid[t, 0] = combine(csrc[t, 0], cdstx.at[t, 0], NX - 1)
        send_all(cmid.at[t, 0], cdstz.at[t, 1], csem.at[t, 2], z_peer, NZ)
        wait_bytes(cdstz.at[t, 0], csem.at[t, 1, 1])
        cmid[t, 1] = combine(csrc[t, 1], cdstz.at[t, 0], NZ - 1)
        send_all(cmid.at[t, 1], cdstx.at[t, 1], csem.at[t, 3], x_peer, NX)
        wait_bytes(cdstz.at[t, 1], csem.at[t, 2, 1])
        first = combine(cmid[t, 0], cdstz.at[t, 1], NZ - 1)
        wait_bytes(cdstx.at[t, 1], csem.at[t, 3, 1])
        second = combine(cmid[t, 1], cdstx.at[t, 1], NX - 1)
        return first, second

    hr = NR // 2
    for h in range(2):
        for b in range(hr):
            rows = pl.ds((h * hr + b) * B, B)
            high = top[rows, :].T
            row_top = jnp.max(high, axis=0, keepdims=True)
            total = jnp.sum(acc[rows, :].T * jnp.exp2(high - row_top), axis=0, keepdims=True)
            rsrc[0, h, b:b + 1, :] = row_top + log2(total)
        rows_out(0, h)

    def widen(h, values):
        for b in range(hr):
            uwide[pl.ds((h * hr + b) * B, B), :] = spread(values[b:b + 1, :])


    fold = (SWEEP // 8, 8, B)
    steps = ROWS // SWEEP // 2
    zeros = (jnp.zeros((8, B), F32),) * NC

    def top_step(i, highs):
        rows = pl.ds(pl.multiple_of(i * SWEEP, SWEEP), SWEEP)
        u = uwide[rows, :]
        return tuple(
            jnp.maximum(high, jnp.max((tile[j, rows, :] + u).reshape(fold), axis=0)) for j, high in enumerate(highs)
        )

    highs = (jnp.full((8, B), -1e30, F32),) * NC
    for h in range(2):
        widen(h, -rows_in(0, h, lse))
        highs = lax.fori_loop(h * steps, (h + 1) * steps, top_step, highs)
    for j in range(NC):
        high = jnp.max(highs[j], axis=0, keepdims=True)
        colm[j:j + 1, :] = high
        high8[j] = jnp.broadcast_to(high - SHIFT, (8, B))

    def exp_step(i, totals):
        rows = pl.ds(pl.multiple_of(i * SWEEP, SWEEP), SWEEP)
        u = uwide[rows, :].reshape(fold)
        sums = []
        for j in range(NC):
            e = jnp.exp2(tile[j, rows, :].reshape(fold) + (u - high8[j]))
            tile[j, rows, :] = e.reshape(SWEEP, B)
            sums.append(totals[j] + jnp.sum(e, axis=0))
        return tuple(sums)

    totals = lax.fori_loop(0, ROWS // SWEEP, exp_step, zeros)
    for j in range(NC):
        colc[j:j + 1, :] = jnp.sum(totals[j], axis=0, keepdims=True)
    hc = NC // 2
    csrc[0] = (colm[...] + (log2(colc[...]) - SHIFT)).reshape(2, hc, B)
    for h, logs in enumerate(over_cols(0, lse)):
        half = pl.ds(h * hc, hc)
        colw[half, :] = jnp.exp2(colm[half, :] - logs + SHIFT)
        colv[half, :] = colw[half, :]

    def iteration(t, carry):
        def rows_pass(i, carry):
            rows = pl.ds(pl.multiple_of(i * 2 * B, 2 * B), 2 * B)
            total = tile[0, rows, :] * colv[0:1, :]
            for j in range(1, NC):
                total = total + tile[j, rows, :] * colv[j:j + 1, :]
            acc[rows, :] = total
            return carry

        for h in range(2):
            lax.fori_loop(h * hr // 2, (h + 1) * hr // 2, rows_pass, 0)
            for b in range(hr):
                rsrc[t, h, b:b + 1, :] = lanes_to_vector(acc[pl.ds((h * hr + b) * B, B), :])
            rows_out(t, h)

        def step(i, totals):
            rows = pl.ds(pl.multiple_of(i * SWEEP, SWEEP), SWEEP)
            u = uwide[rows, :]
            return tuple(
                total + jnp.sum((tile[j, rows, :] * u).reshape(fold), axis=0) for j, total in enumerate(totals)
            )

        totals = zeros
        for h in range(2):
            widen(h, 1.0 / rows_in(t, h, add))
            totals = lax.fori_loop(h * steps, (h + 1) * steps, step, totals)
        for j in range(NC):
            colc[j:j + 1, :] = jnp.sum(totals[j], axis=0, keepdims=True)
        csrc[t] = (colc[...] * colw[...]).reshape(2, hc, B)
        for h, sums in enumerate(over_cols(t, add)):
            half = pl.ds(h * hc, hc)
            colv[half, :] = colw[half, :] / sums
        return carry

    lax.fori_loop(1, ITERS, iteration, 0)

    y = r // 2
    core = lax.rem(r, 2)
    partner = (2 * y + 1 - core, c)

    def target(i):
        return lax.rem(y + 6 - i + 3 * (i // 2) + 2 * (i // 3), NR // 2)

    def weigh(i):
        q = target(i)
        rows = pl.ds(pl.multiple_of(q * 2 * B, 2 * B), 2 * B)
        n = total = None
        for g in range(0, NC, GROUP):
            parts = []
            for j in range(g, g + GROUP):
                w = (tile[j, rows, :] * colv[j:j + 1, :]).astype(BF16)
                parts.append(w)
                wide = w.astype(F32)
                total = wide if total is None else total + wide
            part = jnp.dot(
                jnp.concatenate(parts, axis=1),
                dfull[pl.ds(g, GROUP)].reshape(GROUP * B, D),
                preferred_element_type=F32,
            )
            n = part if n is None else n + part
        for h in range(2):
            num[i, h, 0:B] = n[h * B:(h + 1) * B]
            sums = lanes_to_vector(total[h * B:(h + 1) * B])
            num[i, h, B:B + 8, 0:B] = jnp.broadcast_to(sums, (8, B))
            num[i, h, B:B + 8, B:D] = jnp.zeros((8, B), F32)
        remote(num.at[i, 1 - core], pair.at[i], psem.at[0, i], psem.at[1, i], partner).start()

    def join(i):
        wait_bytes(pair.at[i], psem.at[1, i])
        num[i, core] = num[i, core] + pair[i]

    def hand_over(i):
        join(i)
        q = target(i)
        remote(num.at[i, core], numr.at[i], fsem.at[0], fsem.at[1], (2 * q + core, c)).start()

    def first(i, carry):
        weigh(i)
        return carry

    last = NR // 2 - 1
    lax.fori_loop(0, last, first, 0)
    hand_over(0)
    hand_over(1)
    weigh(last)
    hand_over(2)
    join(last)

    wait_bytes(dfull.at[pl.ds(0, NC - 1)], dsend)
    wait_bytes(nfull.at[pl.ds(0, NR - 1)], nsem.at[0])
    for t in range(ITERS):
        for h in range(2):
            wait_bytes(rdst.at[t, h], rsem.at[t, h, 0])
        wait_bytes(cdstx.at[t, 0], csem.at[t, 0, 0])
        wait_bytes(cdstz.at[t, 0], csem.at[t, 1, 0])
        wait_bytes(cdstz.at[t, 1], csem.at[t, 2, 0])
        wait_bytes(cdstx.at[t, 1], csem.at[t, 3, 0])

    wait_bytes(numr, fsem.at[1])
    total = num[last, core]
    for k in range(last):
        total = total + numr[k]
    scale = spread(total[B:B + 1, 0:B])
    out[:, 0:B] = total[0:B, 0:B] / scale
    out[:, B:D] = total[0:B, B:D] / scale
    wait_bytes(numr, fsem.at[0])
    for i in range(last + 1):
        wait_bytes(pair.at[i], psem.at[0, i])


def solution(mesh):
    vmem, dma = pltpu.VMEM, pltpu.SemaphoreType.DMA
    scratch = [
        vmem((NC, ROWS, B), F32),
        vmem((NC, B, D), BF16),
        vmem((NR, B, D), BF16),
        vmem((ROWS, B), F32),
        vmem((ROWS, B), F32),
        vmem((ROWS, B), F32),
        vmem((NC, B), F32),
        vmem((NC, B), F32),
        vmem((NC, B), F32),
        vmem((NC, B), F32),
        vmem((NC, 8, B), F32),
        vmem((ITERS, 2, NR // 2, B), F32),
        vmem((ITERS, 2, NR - 1, NR // 2, B), F32),
        vmem((ITERS, 2, NC // 2, B), F32),
        vmem((ITERS, 2, NC // 2, B), F32),
        vmem((ITERS, 2, NX - 1, NC // 2, B), F32),
        vmem((ITERS, 2, NZ - 1, NC // 2, B), F32),
        vmem((NR // 2, 2, B + 8, D), F32),
        vmem((NR // 2, B + 8, D), F32),
        vmem((NR // 2 - 1, B + 8, D), F32),
        dma((2,)),
        dma((2,)),
        dma,
        dma((2, NC)),
        dma((ITERS, 2, 2)),
        dma((ITERS, 4, 2)),
        dma((2, NR // 2)),
        dma((2,)),
    ]

    def per_device(noise, data):
        return pl.pallas_call(
            kernel,
            out_shape=jax.ShapeDtypeStruct((B, D), F32),
            in_specs=[pl.BlockSpec(memory_space=pl.ANY)] * 2,
            out_specs=pl.BlockSpec(memory_space=pltpu.VMEM),
            scratch_shapes=scratch,
            compiler_params=pltpu.CompilerParams(
                collective_id=0, has_side_effects=True, vmem_limit_bytes=40 << 20
            ),
        )(noise, data)

    return jax.shard_map(
        per_device,
        mesh=mesh,
        in_specs=(P(("rows", "cols"), None), P(("cols", "rows"), None)),
        out_specs=P(("rows", "cols"), None),
        check_vma=False,
    )
```
